32 devices in a mesh: grp: 2 (over y), ri: 4 (over z), rj: 2 (over x), dp: 2 (over core).
Axes of the slice: x: 2, y: 2, z: 4, core: 2. Of those that a mesh axis runs over, the one named last changes fastest.
Arguments:
- homolog_activations: bfloat16 [64, 128, 256], P(('grp', 'ri', 'rj', 'dp')), parts along dimension 0, may hold values from -6 to 6
- homolog_tallies: int32 [256], P('grp'), parts along dimension 0, may hold values from 8 to 32, as said below
- standardize_gain: float32 [256], replicated, may hold values from 0.25 to 1.75
- standardize_offset: float32 [256], replicated, may hold values from -2.5 to 2.5
- former_factor_matrix: bfloat16 [256, 32], replicated, may hold values from -0.375 to 0.375
- former_factor_offset: float32 [32], replicated, may hold values from -2.5 to 2.5
- latter_factor_matrix: bfloat16 [256, 32], replicated, may hold values from -0.375 to 0.375
- latter_factor_offset: float32 [32], replicated, may hold values from -2.5 to 2.5
- pairwise_projection_matrix: float32 [1024, 128], replicated, may hold values from -3 to 3
Outputs:
- pair_update: float32 [256, 128, 128], P(('grp', 'ri'), ('rj', 'dp')), parts along dimension 0
The draws below stay inside these ranges and needn't reach their ends.
There are 2 independent parts, one for each index of `grp`. The reference program is written for one: setup_inputs(seed, part) draws one part's arguments, and reference() takes and returns one part's arrays. A program takes and returns all parts, laid end to end along the dimension named above; an argument that names none is the same for every part. Nothing has to cross between parts.
Inputs may be any that keep to these rules, and one draw needn't show every extreme that they name: homolog_tallies[r] is the number of live MSA rows of residue r: rows 0 to homolog_tallies[r] - 1 are live, the others masked.
All inputs are finite; a program needn't handle non-finite values.
Results may differ from the reference program's by a relative error of at most 0.0049.
Values may be sent and summed in bfloat16 or wider, within the bound.
No kernel may reach another device: no remote copies, remote signals or barrier semaphores. Data moves between devices by JAX's collectives and lax.ppermute only.
A program may use at most 64 MiB of HBM per device.

```python
import math
import jax
import jax.numpy as jnp
from jax import lax

FEATURE_DEPTH = 256
PANEL_CHANNELS = 32
CZ = 128
HOMOLOG_TOTAL = 32
CHAIN_LENGTH = 128


def draw_homolog_tallies(key, part):
    key = jax.random.fold_in(key, 11)
    leading_key, second_key = jax.random.split(key)
    smallest_row = HOMOLOG_TOTAL // 4
    nonzero_elements = jax.random.randint(leading_key, (CHAIN_LENGTH,), smallest_row, HOMOLOG_TOTAL + 1, dtype=jnp.int32)
    mask_applied = jax.random.randint(second_key, (), 0, CHAIN_LENGTH, dtype=jnp.int32)
    residue_positions = jnp.arange(CHAIN_LENGTH, dtype=jnp.int32)
    nonzero_elements = jnp.where(residue_positions == mask_applied, HOMOLOG_TOTAL, nonzero_elements)
    nonzero_elements = jnp.where(residue_positions == (mask_applied + CHAIN_LENGTH // 2) % CHAIN_LENGTH, smallest_row, nonzero_elements)
    return nonzero_elements


def block_levels(rng, shape, cuts, low, high):
    factor_of, own = 1.0, jax.random.fold_in(rng, 6)
    for position, shards_of in cuts:
        draws = jnp.exp(jax.random.uniform(jax.random.fold_in(own, position), (shards_of,), jnp.float32, low / len(cuts), high / len(cuts)))
        factor_of = factor_of * jnp.repeat(draws, shape[position] // shards_of).reshape([-1 if axis == position else 1 for axis in range(len(shape))])
    return factor_of


def scatter_about(rng, dims, scale, reach, cuts=(), kind=jnp.bfloat16):
    result = scale * jax.random.normal(rng, dims, jnp.float32)
    if cuts:
        result = result * block_levels(rng, dims, cuts, -0.22, 0.18)
    return jnp.clip(result, -reach, reach).astype(kind)


def setup_inputs(seed: int = 0, part: int = 0) -> dict:
    seeds = jax.random.split(jax.random.key(seed), 10)
    part_splits = jax.random.split(jax.random.fold_in(seeds[9], part), 10)
    return {
        "homolog_activations": scatter_about(part_splits[0], (HOMOLOG_TOTAL, CHAIN_LENGTH, FEATURE_DEPTH), 1.0, 6.0, ((0, 16),)),
        "homolog_tallies": draw_homolog_tallies(jax.random.fold_in(jax.random.fold_in(seeds[9], part), 71), part),
        "standardize_gain": jnp.clip(1.0 + 0.15 * jax.random.normal(seeds[2], (FEATURE_DEPTH,), jnp.float32), 0.25, 1.75),
        "standardize_offset": scatter_about(seeds[3], (FEATURE_DEPTH,), 0.3, 2.5, (), jnp.float32),
        "former_factor_matrix": scatter_about(seeds[4], (FEATURE_DEPTH, PANEL_CHANNELS), FEATURE_DEPTH ** -0.5, 0.375),
        "former_factor_offset": scatter_about(seeds[5], (PANEL_CHANNELS,), 0.3, 2.5, (), jnp.float32),
        "latter_factor_matrix": scatter_about(seeds[6], (FEATURE_DEPTH, PANEL_CHANNELS), FEATURE_DEPTH ** -0.5, 0.375),
        "latter_factor_offset": scatter_about(seeds[7], (PANEL_CHANNELS,), 0.3, 2.5, (), jnp.float32),
        "pairwise_projection_matrix": scatter_about(seeds[8], (PANEL_CHANNELS * PANEL_CHANNELS, CZ), 0.5, 3.0, (), jnp.float32),
    }


def reference(homolog_activations, homolog_tallies, standardize_gain, standardize_offset, former_factor_matrix, former_factor_offset, latter_factor_matrix, latter_factor_offset, pairwise_projection_matrix):
    nonzero_elements = homolog_activations.astype(jnp.float32)
    center = nonzero_elements - lax.optimization_barrier(jnp.mean(nonzero_elements, axis=-1, keepdims=True))
    spread = lax.optimization_barrier(jnp.mean(center * center, axis=-1, keepdims=True))
    normalized_input = (center * lax.rsqrt(spread + 1e-05) * standardize_gain + standardize_offset).astype(jnp.bfloat16)
    row_indices = jnp.arange(HOMOLOG_TOTAL, dtype=jnp.int32)
    live = (row_indices[:, None] < homolog_tallies[None, :]).astype(jnp.float32)
    flattened = normalized_input.reshape(HOMOLOG_TOTAL * CHAIN_LENGTH, FEATURE_DEPTH)
    left_panel = jnp.dot(flattened, former_factor_matrix, preferred_element_type=jnp.float32).reshape(HOMOLOG_TOTAL, CHAIN_LENGTH, PANEL_CHANNELS)
    left_panel = ((left_panel + former_factor_offset) * live[:, :, None]).astype(jnp.bfloat16)
    right_panel = jnp.dot(flattened, latter_factor_matrix, preferred_element_type=jnp.float32).reshape(HOMOLOG_TOTAL, CHAIN_LENGTH, PANEL_CHANNELS)
    right_panel = ((right_panel + latter_factor_offset) * live[:, :, None]).astype(jnp.bfloat16)
    right_wide = right_panel.astype(jnp.float32)
    block = math.gcd(CHAIN_LENGTH, 16)

    def one_block(index):
        start = index * block
        piece = lax.dynamic_slice_in_dim(left_panel, start, block, 1).astype(jnp.float32)
        outer = jnp.einsum('sic,sje->ijce', piece, right_wide, precision=lax.Precision.HIGHEST)
        projected = jnp.dot(outer.reshape(block * CHAIN_LENGTH, PANEL_CHANNELS * PANEL_CHANNELS), pairwise_projection_matrix, precision=lax.Precision.HIGHEST).reshape(block, CHAIN_LENGTH, CZ)
        first = lax.dynamic_slice_in_dim(homolog_tallies, start, block, 0)
        bound = jnp.minimum(first[:, None], homolog_tallies[None, :]).astype(jnp.float32)
        return projected / (bound[:, :, None] + 0.001)
    blocks = lax.map(one_block, jnp.arange(CHAIN_LENGTH // block, dtype=jnp.int32))
    return blocks.reshape(CHAIN_LENGTH, CHAIN_LENGTH, CZ)
```

```python
import functools

import jax
import jax.numpy as jnp
from jax import lax
from jax.experimental import pallas as pl
from jax.experimental.pallas import tpu as pltpu
from jax.sharding import PartitionSpec as P

LANES = 128
TILE = 32
ROWS = 16


def span(masks):
    found = [0]
    for mask in masks:
        found += [f ^ mask for f in found]
    return found


def distinct(values):
    return sorted(set(values))


class Plan:
    def __init__(self, masks, split, left_unit, right_unit):
        self.masks = masks
        firsts = lambda ms: distinct(m // split for m in span(ms))
        seconds = lambda ms: distinct(m % split for m in span(ms))
        self.keep, self.send = [], []
        rest = masks[1:]
        left, right = {}, {}
        at = 0
        for p in firsts(rest):
            left[p] = [(0, at)]
            self.keep.append(("L", p))
            at += left_unit
        for p in seconds(rest):
            right[p] = [(0, at)]
            self.keep.append(("R", p))
            at += right_unit
        self.keep_rows = at
        v = masks[0]
        at = 0
        for p in firsts(rest):
            left[p].append((1, at))
            self.send.append(("L", p ^ (v // split)))
            at += left_unit
        for p in seconds(rest):
            right[p].append((1, at))
            self.send.append(("R", p ^ (v % split)))
            at += right_unit
        self.send_rows = at
        self.messages = []
        for step in range(1, len(masks)):
            v, rest = masks[step], masks[step + 1 :]
            message, at, number = [], 0, step + 1
            new_left, new_right = {}, {}
            for p in firsts(rest):
                new_left[p] = list(left[p])
                for buffer, row in left[p ^ (v // split)]:
                    message.append((buffer, row, left_unit))
                    new_left[p].append((number, at))
                    at += left_unit
            for p in seconds(rest):
                new_right[p] = list(right[p])
                for buffer, row in right[p ^ (v % split)]:
                    message.append((buffer, row, right_unit))
                    new_right[p].append((number, at))
                    at += right_unit
            merged = []
            for buffer, row, count in message:
                if merged and merged[-1][0] == buffer and merged[-1][1] + merged[-1][2] == row:
                    merged[-1] = (buffer, merged[-1][1], merged[-1][2] + count)
                else:
                    merged.append((buffer, row, count))
            self.messages.append(merged)
            left, right = new_left, new_right
        self.left, self.right = left[0], right[0]


def panels_kernel(
    plan, split, x_ref, tallies_ref, gain_ref, offset_ref, former_ref, former_bias_ref,
    latter_ref, latter_bias_ref, keep_ref, send_ref, left_ref, right_ref,
):
    depth, chain, features = x_ref.shape
    width = former_ref.shape[1]
    first = lax.axis_index("ri")
    second = lax.axis_index("rj") * lax.axis_size("dp") + lax.axis_index("dp")
    row_start = (first * split + second) * depth

    x = x_ref[...].reshape(depth * chain, features).astype(jnp.float32)
    center = x - jnp.mean(x, axis=-1, keepdims=True)
    spread = jnp.mean(center * center, axis=-1, keepdims=True)
    normed = center * lax.rsqrt(spread + 1e-05) * gain_ref[...] + offset_ref[...]
    normed = normed.astype(jnp.bfloat16)

    copies = LANES // width
    latter = latter_ref[...]
    former = former_ref[...]
    matrix = jnp.concatenate([latter] * copies + [former] * copies, axis=1)
    bias = jnp.concatenate([latter_bias_ref[...]] * copies + [former_bias_ref[...]] * copies, axis=1)
    both = jnp.dot(normed, matrix, preferred_element_type=jnp.float32) + bias

    tallies = tallies_ref[...]
    lane_block = lax.broadcasted_iota(jnp.int32, (8, LANES), 1) // TILE
    for chunk in range(chain // LANES):
        lanes = slice(chunk * LANES, (chunk + 1) * LANES)
        across = jnp.broadcast_to(tallies[:, lanes], (LANES, LANES)).astype(jnp.float32)
        down = across.T
        right_rows, left_rows = [], []
        for s in range(depth):
            row = (row_start + s).astype(jnp.float32)
            rows = slice(s * chain + chunk * LANES, s * chain + (chunk + 1) * LANES)
            right = both[rows, :LANES] * (row < down).astype(jnp.float32)
            left = both[rows, LANES:].T[:width] * (row < across[:width]).astype(jnp.float32)
            right_rows.append(right)
            left_rows.append(left)
        for b in range(LANES // TILE):
            tiles = []
            for s in range(depth):
                tile = None
                for q in range(copies):
                    part = right_rows[s][b * TILE + q * 8 : b * TILE + (q + 1) * 8]
                    tile = part if tile is None else jnp.where(lane_block == q, part, tile)
                tiles.append(tile)
            block = chunk * (LANES // TILE) + b
            right_ref[block * ROWS : (block + 1) * ROWS] = jnp.concatenate(tiles, 0).astype(jnp.bfloat16)
            tiles = []
            for s in range(depth):
                tile = None
                for q in range(copies):
                    part = left_rows[s][q * 8 : (q + 1) * 8]
                    shift = (q - b) * TILE % LANES
                    part = pltpu.roll(part, shift, 1) if shift else part
                    tile = part if tile is None else jnp.where(lane_block == q, part, tile)
                tiles.append(tile)
            left_ref[block * ROWS : (block + 1) * ROWS] = jnp.concatenate(tiles, 0).astype(jnp.bfloat16)

    right_unit = right_ref.shape[0] // split
    for out_ref, pieces in ((keep_ref, plan.keep), (send_ref, plan.send)):
        at = 0
        for kind, position in pieces:
            source, index, unit = (left_ref, first, ROWS) if kind == "L" else (right_ref, second, right_unit)
            start = pl.multiple_of((index ^ position) * unit, ROWS)
            out_ref[at : at + unit] = source[pl.ds(start, unit)]
            at += unit


def pairs_kernel(plan, first_count, second_count, *refs):
    buffers = refs[: len(plan.masks) + 1]
    matrix_ref, down_ref, tallies_ref, out_ref, gather_ref, left_ref, outer_ref, wide_ref = refs[len(plan.masks) + 1 :]
    first = lax.axis_index("ri")
    second = lax.axis_index("rj") * lax.axis_size("dp") + lax.axis_index("dp")
    step = pl.program_id(0)
    sources = len(plan.left)
    depth = sources * 2
    width = LANES // 4

    @pl.when(step == 0)
    def _():
        for k, (buffer, row) in enumerate(plan.left):
            gather_ref[k * ROWS : (k + 1) * ROWS] = buffers[buffer][row : row + ROWS].astype(jnp.float32)
        for half in range(2):
            stacked = jnp.concatenate(
                [gather_ref[pl.ds(half * 4 + c, depth, stride=8)] for c in range(4)], 0
            )
            left_ref[half * LANES : (half + 1) * LANES] = stacked.T.astype(jnp.bfloat16)
        matrix = matrix_ref[...]
        high = matrix.astype(jnp.bfloat16)
        wide_ref[:, :LANES] = high
        wide_ref[:, LANES:] = (matrix - high.astype(jnp.float32)).astype(jnp.bfloat16)

    for k, (buffer, row) in enumerate(plan.right):
        start = pl.multiple_of(row + step * ROWS, ROWS)
        gather_ref[k * ROWS : (k + 1) * ROWS] = buffers[buffer][pl.ds(start, ROWS)].astype(jnp.float32)
    left = left_ref[...]
    lane_block = lax.broadcasted_iota(jnp.int32, (depth, LANES), 1) // width
    for j8 in range(8):
        plain = gather_ref[pl.ds(j8, depth, stride=8)]
        turned = [plain] + [pltpu.roll(plain, r * width, 1) for r in range(1, 4)]
        for pair in range(2):
            columns = []
            for q in (2 * pair, 2 * pair + 1):
                columns.append(
                    jnp.concatenate(
                        [jnp.where(lane_block == c, turned[(c - q) % 4], 0.0) for c in range(4)], 0
                    )
                )
            spread = jnp.concatenate(columns, 1).astype(jnp.bfloat16)
            product = jnp.dot(left, spread, preferred_element_type=jnp.float32).astype(jnp.bfloat16)
            for at, q in enumerate((2 * pair, 2 * pair + 1)):
                j = q * 8 + j8
                for half in range(2):
                    for gq in range(4):
                        rows = (half * 4 + gq) * TILE
                        outer_ref[j * TILE : (j + 1) * TILE, (gq * 2 + half) * LANES : (gq * 2 + half + 1) * LANES] = (
                            product[rows : rows + TILE, at * LANES : (at + 1) * LANES]
                        )
    projected = jnp.dot(outer_ref[...], wide_ref[...], preferred_element_type=jnp.float32)
    projected = projected[:, :LANES] + projected[:, LANES:]
    first_tallies = jnp.broadcast_to(
        down_ref[pl.ds(pl.multiple_of(first * first_count, TILE), first_count)].astype(jnp.float32),
        (first_count, LANES),
    )
    for j in range(TILE):
        other = tallies_ref[second * second_count + step * TILE + j].astype(jnp.float32)
        bound = jnp.minimum(first_tallies, other) + 0.001
        out_ref[pl.ds(j, first_count, stride=TILE)] = projected[j * TILE : (j + 1) * TILE] / bound


def per_device(
    homolog_activations,
    homolog_tallies,
    standardize_gain,
    standardize_offset,
    former_factor_matrix,
    former_factor_offset,
    latter_factor_matrix,
    latter_factor_offset,
    pairwise_projection_matrix,
):
    depth, chain, features = homolog_activations.shape
    size_ri, size_rj, size_dp = (lax.axis_size(a) for a in ("ri", "rj", "dp"))
    split = size_rj * size_dp
    first_count, second_count = chain // size_ri, chain // split
    assert depth == 2 and first_count == TILE and second_count % TILE == 0 and chain % LANES == 0
    left_unit, right_unit = ROWS, ROWS * (second_count // TILE)
    total = size_ri * split
    masks = []
    bit = total // 2
    while bit:
        masks.append(bit if bit < size_dp else bit | (size_dp // 2))
        bit //= 2
    plan = Plan(masks, split, left_unit, right_unit)

    vmem = pl.BlockSpec(memory_space=pltpu.VMEM)
    bf16 = jnp.bfloat16
    keep, send = pl.pallas_call(
        functools.partial(panels_kernel, plan, split),
        out_shape=(
            jax.ShapeDtypeStruct((plan.keep_rows, LANES), bf16),
            jax.ShapeDtypeStruct((plan.send_rows, LANES), bf16),
        ),
        in_specs=[vmem] * 8,
        out_specs=(vmem, vmem),
        scratch_shapes=[
            pltpu.VMEM((chain // TILE * ROWS, LANES), bf16),
            pltpu.VMEM((chain // TILE * ROWS, LANES), bf16),
        ],
        compiler_params=pltpu.CompilerParams(vmem_limit_bytes=32 * 1024 * 1024),
        name="panels",
    )(
        homolog_activations,
        homolog_tallies[None, :],
        standardize_gain[None, :],
        standardize_offset[None, :],
        former_factor_matrix,
        former_factor_offset[None, :],
        latter_factor_matrix,
        latter_factor_offset[None, :],
    )

    axes = ("ri", "rj", "dp")
    swap = lambda v, m: lax.ppermute(v, axes, [(d, d ^ m) for d in range(total)])
    buffers = [keep, swap(send, masks[0])]
    for mask, pieces in zip(masks[1:], plan.messages):
        message = jnp.concatenate([buffers[b][r : r + n] for b, r, n in pieces], 0)
        buffers.append(swap(message, mask))

    blocks = second_count // TILE
    whole = lambda a: pl.BlockSpec(a.shape, lambda j: (0,) * a.ndim)
    down = homolog_tallies[:, None]
    out = pl.pallas_call(
        functools.partial(pairs_kernel, plan, first_count, second_count),
        grid=(blocks,),
        out_shape=jax.ShapeDtypeStruct((blocks, first_count * TILE, LANES), jnp.float32),
        in_specs=[whole(b) for b in buffers]
        + [whole(pairwise_projection_matrix), whole(down), pl.BlockSpec(memory_space=pltpu.SMEM)],
        out_specs=pl.BlockSpec((None, first_count * TILE, LANES), lambda j: (j, 0, 0)),
        scratch_shapes=[
            pltpu.VMEM((total * ROWS, LANES), jnp.float32),
            pltpu.VMEM((2 * LANES, 4 * total * 2), bf16),
            pltpu.VMEM((first_count * TILE, 8 * LANES), bf16),
            pltpu.VMEM((8 * LANES, 2 * LANES), bf16),
        ],
        compiler_params=pltpu.CompilerParams(vmem_limit_bytes=48 * 1024 * 1024),
        name="pairs",
    )(*buffers, pairwise_projection_matrix, down, homolog_tallies)
    out = out.reshape(blocks, first_count, TILE, LANES)
    if blocks == 1:
        return out[0]
    return jnp.transpose(out, (1, 0, 2, 3)).reshape(first_count, second_count, LANES)


def solution(mesh):
    placed = (P(("grp", "ri", "rj", "dp"), None, None), P("grp"), P(), P(), P(), P(), P(), P(), P())
    return jax.shard_map(
        per_device,
        mesh=mesh,
        in_specs=placed,
        out_specs=P(("grp", "ri"), ("rj", "dp"), None),
        check_vma=False,
    )
```

```python
import functools

import jax
import jax.numpy as jnp
from jax import lax
from jax.experimental import pallas as pl
from jax.experimental.pallas import tpu as pltpu
from jax.sharding import PartitionSpec as P

LANES = 128
TILE = 32
ROWS = 16
VMEM_BYTES = 32 * 1024 * 1024


def span(masks):
    found = [0]
    for mask in masks:
        found += [f ^ mask for f in found]
    return found


def distinct(values):
    return sorted(set(values))


class Plan:
    def __init__(self, masks, split, left_unit, right_unit):
        self.masks = masks
        firsts = lambda ms: distinct(m // split for m in span(ms))
        seconds = lambda ms: distinct(m % split for m in span(ms))
        self.keep, self.send = [], []
        rest = masks[1:]
        left, right = {}, {}
        at = 0
        for p in firsts(rest):
            left[p] = [(0, at)]
            self.keep.append(("L", p))
            at += left_unit
        for p in seconds(rest):
            right[p] = [(0, at)]
            self.keep.append(("R", p))
            at += right_unit
        self.keep_rows = at
        v = masks[0]
        at = 0
        for p in firsts(rest):
            left[p].append((1, at))
            self.send.append(("L", p ^ (v // split)))
            at += left_unit
        for p in seconds(rest):
            right[p].append((1, at))
            self.send.append(("R", p ^ (v % split)))
            at += right_unit
        self.send_rows = at
        self.messages = []
        for step in range(1, len(masks)):
            v, rest = masks[step], masks[step + 1 :]
            message, at, number = [], 0, step + 1
            new_left, new_right = {}, {}
            for p in firsts(rest):
                new_left[p] = list(left[p])
                for buffer, row in left[p ^ (v // split)]:
                    message.append((buffer, row, left_unit))
                    new_left[p].append((number, at))
                    at += left_unit
            for p in seconds(rest):
                new_right[p] = list(right[p])
                for buffer, row in right[p ^ (v % split)]:
                    message.append((buffer, row, right_unit))
                    new_right[p].append((number, at))
                    at += right_unit
            merged = []
            for buffer, row, count in message:
                if merged and merged[-1][0] == buffer and merged[-1][1] + merged[-1][2] == row:
                    merged[-1] = (buffer, merged[-1][1], merged[-1][2] + count)
                else:
                    merged.append((buffer, row, count))
            self.messages.append(merged)
            left, right = new_left, new_right
        self.left, self.right = left[0], right[0]


def panels_kernel(
    plan, split, x_hbm, tallies_hbm, gain_hbm, offset_hbm, former_hbm, former_bias_hbm, latter_hbm, latter_bias_hbm,
    matrix_hbm, keep_ref, send_ref, first_ref, second_ref, matrix_ref,
    x_ref, tallies_ref, gain_ref, offset_ref, former_ref, former_bias_ref, latter_ref, latter_bias_ref,
    left_ref, right_ref, down_ref, sems,
):
    depth, chain, features = x_ref.shape
    width = former_ref.shape[0]
    first = lax.axis_index("ri")
    second = lax.axis_index("rj") * lax.axis_size("dp") + lax.axis_index("dp")
    row_start = (first * split + second) * depth

    sources = (x_hbm, latter_hbm, former_hbm, gain_hbm, offset_hbm, tallies_hbm, latter_bias_hbm, former_bias_hbm)
    targets = (x_ref, latter_ref, former_ref, gain_ref, offset_ref, tallies_ref, latter_bias_ref, former_bias_ref)
    copies_in = [pltpu.make_async_copy(a, b, sems.at[k]) for k, (a, b) in enumerate(zip(sources, targets))]
    matrix_copy = pltpu.make_async_copy(matrix_hbm, matrix_ref, sems.at[len(copies_in)])
    for copy in copies_in:
        copy.start()
    matrix_copy.start()
    for copy in copies_in:
        copy.wait()

    x = x_ref[...].reshape(depth * chain, features).astype(jnp.float32)
    center = x - jnp.mean(x, axis=-1, keepdims=True)
    spread = jnp.mean(center * center, axis=-1, keepdims=True)
    normed = center * lax.rsqrt(spread + 1e-05) * gain_ref[...] + offset_ref[...]
    normed = normed.astype(jnp.bfloat16)

    copies = LANES // width
    latter = latter_ref[...]
    former = former_ref[...]
    matrix = jnp.concatenate([latter] * copies + [former] * copies, axis=0)
    bias = jnp.concatenate([latter_bias_ref[...]] * copies + [former_bias_ref[...]] * copies, axis=1)
    both = lax.dot_general(normed, matrix, (((1,), (1,)), ((), ())), preferred_element_type=jnp.float32) + bias

    tallies = tallies_ref[...]
    lane_block = lax.broadcasted_iota(jnp.int32, (8, LANES), 1) // TILE
    for chunk in range(chain // LANES):
        lanes = slice(chunk * LANES, (chunk + 1) * LANES)
        across = jnp.broadcast_to(tallies[:, lanes], (LANES, LANES)).astype(jnp.float32)
        down = across.T
        down_ref[lanes] = down
        right_rows, left_rows = [], []
        for s in range(depth):
            row = (row_start + s).astype(jnp.float32)
            rows = slice(s * chain + chunk * LANES, s * chain + (chunk + 1) * LANES)
            right = both[rows, :LANES] * (row < down).astype(jnp.float32)
            left = both[rows, LANES:].T[:width] * (row < across[:width]).astype(jnp.float32)
            right_rows.append(right)
            left_rows.append(left)
        for b in range(LANES // TILE):
            tiles = []
            for s in range(depth):
                tile = None
                for q in range(copies):
                    part = right_rows[s][b * TILE + q * 8 : b * TILE + (q + 1) * 8]
                    tile = part if tile is None else jnp.where(lane_block == q, part, tile)
                tiles.append(tile)
            block = chunk * (LANES // TILE) + b
            right_ref[block * ROWS : (block + 1) * ROWS] = jnp.concatenate(tiles, 0).astype(jnp.bfloat16)
            tiles = []
            for s in range(depth):
                tile = None
                for q in range(copies):
                    part = left_rows[s][q * 8 : (q + 1) * 8]
                    shift = (q - b) * TILE % LANES
                    part = pltpu.roll(part, shift, 1) if shift else part
                    tile = part if tile is None else jnp.where(lane_block == q, part, tile)
                tiles.append(tile)
            left_ref[block * ROWS : (block + 1) * ROWS] = jnp.concatenate(tiles, 0).astype(jnp.bfloat16)

    right_unit = right_ref.shape[0] // split
    for out_ref, pieces in ((keep_ref, plan.keep), (send_ref, plan.send)):
        at = 0
        for kind, position in pieces:
            source, index, unit = (left_ref, first, ROWS) if kind == "L" else (right_ref, second, right_unit)
            start = pl.multiple_of((index ^ position) * unit, ROWS)
            out_ref[at : at + unit] = source[pl.ds(start, unit)]
            at += unit
    for out_ref, index in ((first_ref, first), (second_ref, second)):
        count = out_ref.shape[0]
        out_ref[...] = down_ref[pl.ds(pl.multiple_of(index * count, TILE), count)]
    matrix_copy.wait()


def pairs_kernel(plan, first_count, second_count, *refs):
    buffers = refs[: len(plan.masks) + 1]
    matrix_ref, first_ref, second_ref, out_ref, gather_ref, left_ref, outer_ref, wide_ref = refs[len(plan.masks) + 1 :]
    sources = len(plan.left)
    depth = sources * 2
    width = LANES // 4

    for k, (buffer, row) in enumerate(plan.left):
        gather_ref[k * ROWS : (k + 1) * ROWS] = buffers[buffer][row : row + ROWS].astype(jnp.float32)
    for half in range(2):
        stacked = jnp.concatenate([gather_ref[pl.ds(half * 4 + c, depth, stride=8)] for c in range(4)], 0)
        left_ref[half * LANES : (half + 1) * LANES] = stacked.T.astype(jnp.bfloat16)
    matrix = matrix_ref[...]
    high = matrix.astype(jnp.bfloat16)
    wide_ref[:, :LANES] = high
    wide_ref[:, LANES:] = (matrix - high.astype(jnp.float32)).astype(jnp.bfloat16)
    first_tallies = first_ref[...]

    def one_block(block, carry):
        for k, (buffer, row) in enumerate(plan.right):
            start = pl.multiple_of(row + block * ROWS, ROWS)
            gather_ref[k * ROWS : (k + 1) * ROWS] = buffers[buffer][pl.ds(start, ROWS)].astype(jnp.float32)
        left = left_ref[...]
        lane_block = lax.broadcasted_iota(jnp.int32, (depth, LANES), 1) // width
        for j8 in range(8):
            plain = gather_ref[pl.ds(j8, depth, stride=8)]
            turned = [plain] + [pltpu.roll(plain, r * width, 1) for r in range(1, 4)]
            for pair in range(2):
                columns = []
                for q in (2 * pair, 2 * pair + 1):
                    columns.append(
                        jnp.concatenate([jnp.where(lane_block == c, turned[(c - q) % 4], 0.0) for c in range(4)], 0)
                    )
                spread = jnp.concatenate(columns, 1).astype(jnp.bfloat16)
                product = jnp.dot(left, spread, preferred_element_type=jnp.float32).astype(jnp.bfloat16)
                for at, q in enumerate((2 * pair, 2 * pair + 1)):
                    j = q * 8 + j8
                    for half in range(2):
                        for gq in range(4):
                            rows = (half * 4 + gq) * TILE
                            group = gq * 2 + half
                            outer_ref[j * TILE : (j + 1) * TILE, group * LANES : (group + 1) * LANES] = (
                                product[rows : rows + TILE, at * LANES : (at + 1) * LANES]
                            )
        projected = jnp.dot(outer_ref[...], wide_ref[...], preferred_element_type=jnp.float32)
        projected = projected[:, :LANES] + projected[:, LANES:]
        for j in range(TILE):
            at = block * TILE + j
            bound = jnp.minimum(first_tallies, second_ref[pl.ds(at, 1)]) + 0.001
            out_ref[pl.ds(at, first_count, stride=second_count)] = projected[j * TILE : (j + 1) * TILE] / bound
        return carry

    blocks = second_count // TILE
    if blocks == 1:
        one_block(0, 0)
    else:
        lax.fori_loop(0, blocks, one_block, 0)


def per_device(
    homolog_activations,
    homolog_tallies,
    standardize_gain,
    standardize_offset,
    former_factor_matrix,
    former_factor_offset,
    latter_factor_matrix,
    latter_factor_offset,
    pairwise_projection_matrix,
):
    depth, chain, features = homolog_activations.shape
    size_ri, size_rj, size_dp = (lax.axis_size(a) for a in ("ri", "rj", "dp"))
    split = size_rj * size_dp
    first_count, second_count = chain // size_ri, chain // split
    assert depth == 2 and first_count == TILE and second_count % TILE == 0 and chain % LANES == 0
    left_unit, right_unit = ROWS, ROWS * (second_count // TILE)
    total = size_ri * split
    masks = []
    bit = total // 2
    while bit:
        masks.append(bit if bit < size_dp else bit | (size_dp // 2))
        bit //= 2
    plan = Plan(masks, split, left_unit, right_unit)

    vmem = pl.BlockSpec(memory_space=pltpu.VMEM)
    bf16, f32 = jnp.bfloat16, jnp.float32
    operands = (
        homolog_activations,
        homolog_tallies[None, :],
        standardize_gain[None, :],
        standardize_offset[None, :],
        former_factor_matrix.T,
        former_factor_offset[None, :],
        latter_factor_matrix.T,
        latter_factor_offset[None, :],
    )
    in_hbm = [pltpu.with_memory_space_constraint(a, pltpu.HBM) for a in operands + (pairwise_projection_matrix,)]
    keep, send, first_tallies, second_tallies, matrix = pl.pallas_call(
        functools.partial(panels_kernel, plan, split),
        out_shape=(
            jax.ShapeDtypeStruct((plan.keep_rows, LANES), bf16),
            jax.ShapeDtypeStruct((plan.send_rows, LANES), bf16),
            jax.ShapeDtypeStruct((first_count, LANES), f32),
            jax.ShapeDtypeStruct((second_count, LANES), f32),
            jax.ShapeDtypeStruct(pairwise_projection_matrix.shape, f32),
        ),
        in_specs=[pl.BlockSpec(memory_space=pltpu.HBM)] * len(in_hbm),
        out_specs=(vmem,) * 5,
        scratch_shapes=[pltpu.VMEM(a.shape, a.dtype) for a in operands]
        + [
            pltpu.VMEM((chain // TILE * ROWS, LANES), bf16),
            pltpu.VMEM((chain // TILE * ROWS, LANES), bf16),
            pltpu.VMEM((chain, LANES), f32),
            pltpu.SemaphoreType.DMA((len(in_hbm),)),
        ],
        compiler_params=pltpu.CompilerParams(vmem_limit_bytes=VMEM_BYTES),
        name="panels",
    )(*in_hbm)

    axes = ("ri", "rj", "dp")
    swap = lambda v, m: lax.ppermute(v, axes, [(d, d ^ m) for d in range(total)])
    buffers = [keep, swap(send, masks[0])]
    for mask, pieces in zip(masks[1:], plan.messages):
        message = jnp.concatenate([buffers[b][r : r + n] for b, r, n in pieces], 0)
        buffers.append(swap(message, mask))

    out = pl.pallas_call(
        functools.partial(pairs_kernel, plan, first_count, second_count),
        out_shape=jax.ShapeDtypeStruct((first_count * second_count, LANES), f32),
        in_specs=[vmem] * (len(buffers) + 3),
        out_specs=vmem,
        scratch_shapes=[
            pltpu.VMEM((total * ROWS, LANES), f32),
            pltpu.VMEM((2 * LANES, 4 * total * 2), bf16),
            pltpu.VMEM((first_count * TILE, 8 * LANES), bf16),
            pltpu.VMEM((8 * LANES, 2 * LANES), bf16),
        ],
        compiler_params=pltpu.CompilerParams(vmem_limit_bytes=VMEM_BYTES),
        name="pairs",
    )(*buffers, matrix, first_tallies, second_tallies)
    return out.reshape(first_count, second_count, LANES)


def solution(mesh):
    placed = (P(("grp", "ri", "rj", "dp"), None, None), P("grp"), P(), P(), P(), P(), P(), P(), P())
    return jax.shard_map(
        per_device,
        mesh=mesh,
        in_specs=placed,
        out_specs=P(("grp", "ri"), ("rj", "dp"), None),
        check_vma=False,
    )
```

```python
import functools

import jax
import jax.numpy as jnp
from jax import lax
from jax.experimental import pallas as pl
from jax.experimental.pallas import tpu as pltpu
from jax.sharding import PartitionSpec as P

LANES = 128
TILE = 32
ROWS = 16
VMEM_BYTES = 32 * 1024 * 1024


def distinct(values):
    return sorted(set(values))


def reach(stages):
    found = [0]
    for masks in stages:
        found = [f ^ m for m in [0] + masks for f in found]
    return found


class Plan:
    def __init__(self, stages, split, left_unit, right_unit):
        firsts = lambda s: distinct(m // split for m in reach(s))
        seconds = lambda s: distinct(m % split for m in reach(s))
        left, right, self.own, self.rows = {}, {}, [], 0
        for kind, held, positions, unit in (
            ("L", left, firsts(stages), left_unit),
            ("R", right, seconds(stages), right_unit),
        ):
            for p in positions:
                held[p] = [(0, self.rows)]
                self.own.append((kind, p))
                self.rows += unit
        self.messages, buffer = [], 0
        for stage, masks in enumerate(stages):
            rest = stages[stage + 1 :]
            new_left = {p: list(left[p]) for p in firsts(rest)}
            new_right = {p: list(right[p]) for p in seconds(rest)}
            for mask in masks:
                buffer += 1
                message, at = [], 0
                for new, old, shift, unit in (
                    (new_left, left, mask // split, left_unit),
                    (new_right, right, mask % split, right_unit),
                ):
                    for p in new:
                        for source, row in old[p ^ shift]:
                            if message and message[-1][0] == source and sum(message[-1][1:]) == row:
                                message[-1] = (source, message[-1][1], message[-1][2] + unit)
                            else:
                                message.append((source, row, unit))
                            new[p].append((buffer, at))
                            at += unit
                self.messages.append((stage, mask, message))
            left, right = new_left, new_right
        self.buffers = buffer + 1
        self.left, self.right = left[0], right[0]


def panels_kernel(
    plan, split, x_hbm, tallies_hbm, gain_hbm, offset_hbm, former_hbm, former_bias_hbm, latter_hbm, latter_bias_hbm,
    matrix_hbm, *refs,
):
    sends = sum(stage == 0 for stage, _, _ in plan.messages)
    own_ref, *send_refs = refs[: 1 + sends]
    first_ref, second_ref, matrix_ref = refs[1 + sends : 4 + sends]
    x_ref, tallies_ref, gain_ref, offset_ref, former_ref, former_bias_ref, latter_ref, latter_bias_ref = refs[4 + sends : 12 + sends]
    left_ref, right_ref, down_ref, sems = refs[12 + sends :]
    depth, chain, features = x_ref.shape
    width = former_ref.shape[0]
    first = lax.axis_index("ri")
    second = lax.axis_index("rj") * lax.axis_size("dp") + lax.axis_index("dp")
    row_start = (first * split + second) * depth

    sources = (x_hbm, latter_hbm, former_hbm, gain_hbm, offset_hbm, tallies_hbm, latter_bias_hbm, former_bias_hbm)
    targets = (x_ref, latter_ref, former_ref, gain_ref, offset_ref, tallies_ref, latter_bias_ref, former_bias_ref)
    copies_in = [pltpu.make_async_copy(a, b, sems.at[k]) for k, (a, b) in enumerate(zip(sources, targets))]
    matrix_copy = pltpu.make_async_copy(matrix_hbm, matrix_ref, sems.at[len(copies_in)])
    for copy in copies_in:
        copy.start()
    matrix_copy.start()
    for copy in copies_in:
        copy.wait()

    x = x_ref[...].reshape(depth * chain, features).astype(jnp.float32)
    center = x - jnp.mean(x, axis=-1, keepdims=True)
    spread = jnp.mean(center * center, axis=-1, keepdims=True)
    normed = center * lax.rsqrt(spread + 1e-05) * gain_ref[...] + offset_ref[...]
    normed = normed.astype(jnp.bfloat16)

    copies = LANES // width
    latter = latter_ref[...]
    former = former_ref[...]
    matrix = jnp.concatenate([latter] * copies + [former] * copies, axis=0)
    bias = jnp.concatenate([latter_bias_ref[...]] * copies + [former_bias_ref[...]] * copies, axis=1)
    both = lax.dot_general(normed, matrix, (((1,), (1,)), ((), ())), preferred_element_type=jnp.float32) + bias

    tallies = tallies_ref[...]
    lane_block = lax.broadcasted_iota(jnp.int32, (8, LANES), 1) // TILE
    for chunk in range(chain // LANES):
        lanes = slice(chunk * LANES, (chunk + 1) * LANES)
        across = jnp.broadcast_to(tallies[:, lanes], (LANES, LANES)).astype(jnp.float32)
        down = across.T
        down_ref[lanes] = down
        right_rows, left_rows = [], []
        for s in range(depth):
            row = (row_start + s).astype(jnp.float32)
            rows = slice(s * chain + chunk * LANES, s * chain + (chunk + 1) * LANES)
            right = both[rows, :LANES] * (row < down).astype(jnp.float32)
            left = both[rows, LANES:].T[:width] * (row < across[:width]).astype(jnp.float32)
            right_rows.append(right)
            left_rows.append(left)
        for b in range(LANES // TILE):
            tiles = []
            for s in range(depth):
                tile = None
                for q in range(copies):
                    part = right_rows[s][b * TILE + q * 8 : b * TILE + (q + 1) * 8]
                    tile = part if tile is None else jnp.where(lane_block == q, part, tile)
                tiles.append(tile)
            block = chunk * (LANES // TILE) + b
            right_ref[block * ROWS : (block + 1) * ROWS] = jnp.concatenate(tiles, 0).astype(jnp.bfloat16)
            tiles = []
            for s in range(depth):
                tile = None
                for q in range(copies):
                    part = left_rows[s][q * 8 : (q + 1) * 8]
                    shift = (q - b) * TILE % LANES
                    part = pltpu.roll(part, shift, 1) if shift else part
                    tile = part if tile is None else jnp.where(lane_block == q, part, tile)
                tiles.append(tile)
            left_ref[block * ROWS : (block + 1) * ROWS] = jnp.concatenate(tiles, 0).astype(jnp.bfloat16)

    right_unit = right_ref.shape[0] // split
    at = 0
    for kind, position in plan.own:
        source, index, unit = (left_ref, first, ROWS) if kind == "L" else (right_ref, second, right_unit)
        start = pl.multiple_of((index ^ position) * unit, ROWS)
        own_ref[at : at + unit] = source[pl.ds(start, unit)]
        at += unit
    for send_ref, (_, _, message) in zip(send_refs, plan.messages):
        at = 0
        for _, row, count in message:
            send_ref[at : at + count] = own_ref[row : row + count]
            at += count
    for out_ref, index in ((first_ref, first), (second_ref, second)):
        count = out_ref.shape[0]
        out_ref[...] = down_ref[pl.ds(pl.multiple_of(index * count, TILE), count)]
    matrix_copy.wait()


def pairs_kernel(plan, first_count, second_count, *refs):
    buffers = refs[: plan.buffers]
    matrix_ref, first_ref, second_ref, out_ref, gather_ref, left_ref, outer_ref, wide_ref = refs[plan.buffers :]
    sources = len(plan.left)
    depth = sources * 2
    width = LANES // 4

    for k, (buffer, row) in enumerate(plan.left):
        gather_ref[k * ROWS : (k + 1) * ROWS] = buffers[buffer][row : row + ROWS].astype(jnp.float32)
    for half in range(2):
        stacked = jnp.concatenate([gather_ref[pl.ds(half * 4 + c, depth, stride=8)] for c in range(4)], 0)
        left_ref[half * LANES : (half + 1) * LANES] = stacked.T.astype(jnp.bfloat16)
    matrix = matrix_ref[...]
    high = matrix.astype(jnp.bfloat16)
    wide_ref[:, :LANES] = high
    wide_ref[:, LANES:] = (matrix - high.astype(jnp.float32)).astype(jnp.bfloat16)
    first_tallies = first_ref[...]

    def one_block(block, carry):
        for k, (buffer, row) in enumerate(plan.right):
            start = pl.multiple_of(row + block * ROWS, ROWS)
            gather_ref[k * ROWS : (k + 1) * ROWS] = buffers[buffer][pl.ds(start, ROWS)].astype(jnp.float32)
        left = left_ref[...]
        lane_block = lax.broadcasted_iota(jnp.int32, (depth, LANES), 1) // width
        for j8 in range(8):
            plain = gather_ref[pl.ds(j8, depth, stride=8)]
            turned = [plain] + [pltpu.roll(plain, r * width, 1) for r in range(1, 4)]
            for pair in range(2):
                columns = []
                for q in (2 * pair, 2 * pair + 1):
                    columns.append(
                        jnp.concatenate([jnp.where(lane_block == c, turned[(c - q) % 4], 0.0) for c in range(4)], 0)
                    )
                spread = jnp.concatenate(columns, 1).astype(jnp.bfloat16)
                product = jnp.dot(left, spread, preferred_element_type=jnp.float32).astype(jnp.bfloat16)
                for at, q in enumerate((2 * pair, 2 * pair + 1)):
                    j = q * 8 + j8
                    for half in range(2):
                        for gq in range(4):
                            rows = (half * 4 + gq) * TILE
                            group = gq * 2 + half
                            outer_ref[j * TILE : (j + 1) * TILE, group * LANES : (group + 1) * LANES] = (
                                product[rows : rows + TILE, at * LANES : (at + 1) * LANES]
                            )
        projected = jnp.dot(outer_ref[...], wide_ref[...], preferred_element_type=jnp.float32)
        projected = projected[:, :LANES] + projected[:, LANES:]
        for j in range(TILE):
            at = block * TILE + j
            bound = jnp.minimum(first_tallies, second_ref[pl.ds(at, 1)]) + 0.001
            out_ref[pl.ds(at, first_count, stride=second_count)] = projected[j * TILE : (j + 1) * TILE] / bound
        return carry

    blocks = second_count // TILE
    if blocks == 1:
        one_block(0, 0)
    else:
        lax.fori_loop(0, blocks, one_block, 0)


def per_device(
    homolog_activations,
    homolog_tallies,
    standardize_gain,
    standardize_offset,
    former_factor_matrix,
    former_factor_offset,
    latter_factor_matrix,
    latter_factor_offset,
    pairwise_projection_matrix,
):
    depth, chain, features = homolog_activations.shape
    size_ri, size_rj, size_dp = (lax.axis_size(a) for a in ("ri", "rj", "dp"))
    split = size_rj * size_dp
    first_count, second_count = chain // size_ri, chain // split
    assert depth == 2 and first_count == TILE and second_count % TILE == 0 and chain % LANES == 0
    left_unit, right_unit = ROWS, ROWS * (second_count // TILE)
    total = size_ri * split
    bits = []
    bit = total // 2
    while bit >= size_dp:
        bits.append(bit)
        bit //= 2
    core = size_dp // 2
    stages = [[bits[0] | core]] if len(bits) % 2 else []
    bits = bits[len(bits) % 2 :]
    for high, low in zip(bits[::2], bits[1::2]):
        stages.append([low | core, high | core, low | high])
    if core:
        stages.append([core])
    plan = Plan(stages, split, left_unit, right_unit)
    sent = [sum(count for _, _, count in message) for stage, _, message in plan.messages if stage == 0]

    vmem = pl.BlockSpec(memory_space=pltpu.VMEM)
    bf16, f32 = jnp.bfloat16, jnp.float32
    operands = (
        homolog_activations,
        homolog_tallies[None, :],
        standardize_gain[None, :],
        standardize_offset[None, :],
        former_factor_matrix.T,
        former_factor_offset[None, :],
        latter_factor_matrix.T,
        latter_factor_offset[None, :],
    )
    in_hbm = [pltpu.with_memory_space_constraint(a, pltpu.HBM) for a in operands + (pairwise_projection_matrix,)]
    *own, first_tallies, second_tallies, matrix = pl.pallas_call(
        functools.partial(panels_kernel, plan, split),
        out_shape=(
            *(jax.ShapeDtypeStruct((rows, LANES), bf16) for rows in [plan.rows] + sent),
            jax.ShapeDtypeStruct((first_count, LANES), f32),
            jax.ShapeDtypeStruct((second_count, LANES), f32),
            jax.ShapeDtypeStruct(pairwise_projection_matrix.shape, f32),
        ),
        in_specs=[pl.BlockSpec(memory_space=pltpu.HBM)] * len(in_hbm),
        out_specs=(vmem,) * (4 + len(sent)),
        scratch_shapes=[pltpu.VMEM(a.shape, a.dtype) for a in operands]
        + [
            pltpu.VMEM((chain // TILE * ROWS, LANES), bf16),
            pltpu.VMEM((chain // TILE * ROWS, LANES), bf16),
            pltpu.VMEM((chain, LANES), f32),
            pltpu.SemaphoreType.DMA((len(in_hbm),)),
        ],
        compiler_params=pltpu.CompilerParams(vmem_limit_bytes=VMEM_BYTES),
        name="panels",
    )(*in_hbm)

    axes = ("ri", "rj", "dp")
    swap = lambda v, m: lax.ppermute(v, axes, [(d, d ^ m) for d in range(total)])
    buffers = own[:1]
    stage_of = lambda s: [(mask, message) for stage, mask, message in plan.messages if stage == s]
    for s in range(len(stages)):
        if s == 0:
            messages = own[1:]
        else:
            messages = [jnp.concatenate([buffers[b][r : r + n] for b, r, n in m], 0) for _, m in stage_of(s)]
        buffers = buffers + [swap(v, mask) for v, (mask, _) in zip(messages, stage_of(s))]

    out = pl.pallas_call(
        functools.partial(pairs_kernel, plan, first_count, second_count),
        out_shape=jax.ShapeDtypeStruct((first_count * second_count, LANES), f32),
        in_specs=[vmem] * (len(buffers) + 3),
        out_specs=vmem,
        scratch_shapes=[
            pltpu.VMEM((total * ROWS, LANES), f32),
            pltpu.VMEM((2 * LANES, 4 * total * 2), bf16),
            pltpu.VMEM((first_count * TILE, 8 * LANES), bf16),
            pltpu.VMEM((8 * LANES, 2 * LANES), bf16),
        ],
        compiler_params=pltpu.CompilerParams(vmem_limit_bytes=VMEM_BYTES),
        name="pairs",
    )(*buffers, matrix, first_tallies, second_tallies)
    return out.reshape(first_count, second_count, LANES)


def solution(mesh):
    placed = (P(("grp", "ri", "rj", "dp"), None, None), P("grp"), P(), P(), P(), P(), P(), P(), P())
    return jax.shard_map(
        per_device,
        mesh=mesh,
        in_specs=placed,
        out_specs=P(("grp", "ri"), ("rj", "dp"), None),
        check_vma=False,
    )
```

```python
import functools

import jax
import jax.numpy as jnp
from jax import lax
from jax.experimental import pallas as pl
from jax.experimental.pallas import tpu as pltpu
from jax.sharding import PartitionSpec as P

LANES = 128
TILE = 32
ROWS = 16
VMEM_BYTES = 32 * 1024 * 1024


def distinct(values):
    return sorted(set(values))


def reach(stages):
    found = [0]
    for masks in stages:
        found = [f ^ m for m in [0] + masks for f in found]
    return found


class Plan:
    def __init__(self, stages, split, left_unit, right_unit):
        firsts = lambda s: distinct(m // split for m in reach(s))
        seconds = lambda s: distinct(m % split for m in reach(s))
        left, right, self.own, self.rows = {}, {}, [], 0
        for kind, held, positions, unit in (
            ("L", left, firsts(stages), left_unit),
            ("R", right, seconds(stages), right_unit),
        ):
            for p in positions:
                held[p] = [(0, self.rows)]
                self.own.append((kind, p))
                self.rows += unit
        self.messages, buffer = [], 0
        for stage, masks in enumerate(stages):
            rest = stages[stage + 1 :]
            new_left = {p: list(left[p]) for p in firsts(rest)}
            new_right = {p: list(right[p]) for p in seconds(rest)}
            for mask in masks:
                buffer += 1
                message, at = [], 0
                for new, old, shift, unit in (
                    (new_left, left, mask // split, left_unit),
                    (new_right, right, mask % split, right_unit),
                ):
                    for p in new:
                        for source, row in old[p ^ shift]:
                            if message and message[-1][0] == source and sum(message[-1][1:]) == row:
                                message[-1] = (source, message[-1][1], message[-1][2] + unit)
                            else:
                                message.append((source, row, unit))
                            new[p].append((buffer, at))
                            at += unit
                self.messages.append((stage, mask, message))
            left, right = new_left, new_right
        self.buffers = buffer + 1
        self.left, self.right = left[0], right[0]


def panels_kernel(
    plan, split, x_hbm, tallies_hbm, gain_hbm, offset_hbm, former_hbm, former_bias_hbm, latter_hbm, latter_bias_hbm,
    matrix_hbm, *refs,
):
    sends = sum(stage == 0 for stage, _, _ in plan.messages)
    own_ref, *send_refs = refs[: 1 + sends]
    first_ref, second_ref, matrix_ref = refs[1 + sends : 4 + sends]
    x_ref, tallies_ref, gain_ref, offset_ref, former_ref, former_bias_ref, latter_ref, latter_bias_ref = refs[4 + sends : 12 + sends]
    left_ref, right_ref, down_ref, sems = refs[12 + sends :]
    depth, chain, features = x_ref.shape
    width = former_ref.shape[0]
    first = lax.axis_index("ri")
    second = lax.axis_index("rj") * lax.axis_size("dp") + lax.axis_index("dp")
    row_start = (first * split + second) * depth

    sources = (x_hbm, latter_hbm, former_hbm, gain_hbm, offset_hbm, tallies_hbm, latter_bias_hbm, former_bias_hbm)
    targets = (x_ref, latter_ref, former_ref, gain_ref, offset_ref, tallies_ref, latter_bias_ref, former_bias_ref)
    copies_in = [pltpu.make_async_copy(a, b, sems.at[k]) for k, (a, b) in enumerate(zip(sources, targets))]
    matrix_copy = pltpu.make_async_copy(matrix_hbm, matrix_ref, sems.at[len(copies_in)])
    for copy in copies_in:
        copy.start()
    matrix_copy.start()
    for copy in copies_in:
        copy.wait()

    x = x_ref[...].reshape(depth * chain, features).astype(jnp.float32)
    center = x - jnp.mean(x, axis=-1, keepdims=True)
    spread = jnp.mean(center * center, axis=-1, keepdims=True)
    normed = center * lax.rsqrt(spread + 1e-05) * gain_ref[...] + offset_ref[...]
    normed = normed.astype(jnp.bfloat16)

    copies = LANES // width
    latter = latter_ref[...]
    former = former_ref[...]
    matrix = jnp.concatenate([latter] * copies + [former] * copies, axis=0)
    bias = jnp.concatenate([latter_bias_ref[...]] * copies + [former_bias_ref[...]] * copies, axis=1)
    both = lax.dot_general(normed, matrix, (((1,), (1,)), ((), ())), preferred_element_type=jnp.float32) + bias

    tallies = tallies_ref[...]
    lane_block = lax.broadcasted_iota(jnp.int32, (8, LANES), 1) // TILE
    for chunk in range(chain // LANES):
        lanes = slice(chunk * LANES, (chunk + 1) * LANES)
        across = jnp.broadcast_to(tallies[:, lanes], (LANES, LANES)).astype(jnp.float32)
        down = across.T
        down_ref[lanes] = down
        right_rows, left_rows = [], []
        for s in range(depth):
            row = (row_start + s).astype(jnp.float32)
            rows = slice(s * chain + chunk * LANES, s * chain + (chunk + 1) * LANES)
            right = both[rows, :LANES] * (row < down).astype(jnp.float32)
            left = both[rows, LANES:].T[:width] * (row < across[:width]).astype(jnp.float32)
            right_rows.append(right)
            left_rows.append(left)
        for b in range(LANES // TILE):
            tiles = []
            for s in range(depth):
                tile = None
                for q in range(copies):
                    part = right_rows[s][b * TILE + q * 8 : b * TILE + (q + 1) * 8]
                    tile = part if tile is None else jnp.where(lane_block == q, part, tile)
                tiles.append(tile)
            block = chunk * (LANES // TILE) + b
            right_ref[block * ROWS : (block + 1) * ROWS] = jnp.concatenate(tiles, 0).astype(jnp.bfloat16)
            tiles = []
            for s in range(depth):
                tile = None
                for q in range(copies):
                    part = left_rows[s][q * 8 : (q + 1) * 8]
                    shift = (q - b) * TILE % LANES
                    part = pltpu.roll(part, shift, 1) if shift else part
                    tile = part if tile is None else jnp.where(lane_block == q, part, tile)
                tiles.append(tile)
            left_ref[block * ROWS : (block + 1) * ROWS] = jnp.concatenate(tiles, 0).astype(jnp.bfloat16)

    right_unit = right_ref.shape[0] // split
    at = 0
    for kind, position in plan.own:
        source, index, unit = (left_ref, first, ROWS) if kind == "L" else (right_ref, second, right_unit)
        start = pl.multiple_of((index ^ position) * unit, ROWS)
        own_ref[at : at + unit] = source[pl.ds(start, unit)]
        at += unit
    for send_ref, (_, _, message) in zip(send_refs, plan.messages):
        at = 0
        for _, row, count in message:
            send_ref[at : at + count] = own_ref[row : row + count]
            at += count
    for out_ref, index in ((first_ref, first), (second_ref, second)):
        count = out_ref.shape[0]
        out_ref[...] = 1.0 / (down_ref[pl.ds(pl.multiple_of(index * count, TILE), count)] + 0.001)
    matrix_copy.wait()


def pairs_kernel(plan, *refs):
    buffers = refs[: plan.buffers]
    matrix_ref, first_ref, second_ref, out_ref = refs[plan.buffers : plan.buffers + 4]
    gather_ref, left_ref, outer_ref, wide_ref, done_ref, sems = refs[plan.buffers + 4 :]
    first_count, second_count, _ = out_ref.shape
    sources = len(plan.left)
    depth = sources * 2
    width = LANES // 4

    for k, (buffer, row) in enumerate(plan.left):
        gather_ref[k * ROWS : (k + 1) * ROWS] = buffers[buffer][row : row + ROWS].astype(jnp.float32)
    for half in range(2):
        stacked = jnp.concatenate([gather_ref[pl.ds(half * 4 + c, depth, stride=8)] for c in range(4)], 0)
        left_ref[half * LANES : (half + 1) * LANES] = stacked.T.astype(jnp.bfloat16)
    matrix = matrix_ref[...]
    high = matrix.astype(jnp.bfloat16)
    wide_ref[:, :LANES] = high
    wide_ref[:, LANES:] = (matrix - high.astype(jnp.float32)).astype(jnp.bfloat16)
    first_scale = first_ref[...]

    def one_block(block, carry):
        for k, (buffer, row) in enumerate(plan.right):
            start = pl.multiple_of(row + block * ROWS, ROWS)
            at = (sources + k) * ROWS
            gather_ref[at : at + ROWS] = buffers[buffer][pl.ds(start, ROWS)].astype(jnp.float32)
        left = left_ref[...]
        lane_block = lax.broadcasted_iota(jnp.int32, (depth, LANES), 1) // width
        zero = jnp.zeros((depth, LANES), jnp.bfloat16)
        turned = []
        for j8 in range(8):
            plain = gather_ref[pl.ds(sources * ROWS + j8, depth, stride=8)]
            turned.append([(pltpu.roll(plain, r * width, 1) if r else plain).astype(jnp.bfloat16) for r in range(4)])

        def outer(q):
            for j8 in range(0, 8, 2):
                spread = jnp.concatenate(
                    [
                        jnp.concatenate([jnp.where(lane_block == c, t[(c - q) % 4], zero) for c in range(4)], 0)
                        for t in turned[j8 : j8 + 2]
                    ],
                    1,
                )
                product = jnp.dot(left, spread, preferred_element_type=jnp.float32).astype(jnp.bfloat16)
                for at in range(2):
                    j = q * 8 + j8 + at
                    for half in range(2):
                        for gq in range(4):
                            rows = (half * 4 + gq) * TILE
                            group = gq * 2 + half
                            outer_ref[j * TILE : (j + 1) * TILE, group * LANES : (group + 1) * LANES] = (
                                product[rows : rows + TILE, at * LANES : (at + 1) * LANES]
                            )

        def project(q):
            rows = outer_ref[q * 8 * TILE : (q + 1) * 8 * TILE]
            projected = jnp.dot(rows, wide_ref[...], preferred_element_type=jnp.float32)
            projected = projected[:, :LANES] + projected[:, LANES:]
            start = pl.multiple_of(block * TILE + q * 8, 8)
            for k in range(8):
                scale = jnp.maximum(first_scale, second_ref[pl.ds(start + k, 1)])
                done_ref[q, pl.ds(k, first_count, stride=8)] = projected[k * TILE : (k + 1) * TILE] * scale
            return pltpu.make_async_copy(
                done_ref.at[q].reshape(first_count, 8, LANES), out_ref.at[:, pl.ds(start, 8)], sems.at[q]
            )

        outer(0)
        outer(1)
        copies = []
        for q in range(4):
            if q + 2 < 4:
                outer(q + 2)
            copies.append(project(q))
            copies[-1].start()
        for copy in copies:
            copy.wait()
        return carry

    blocks = second_count // TILE
    if blocks == 1:
        one_block(0, 0)
    else:
        lax.fori_loop(0, blocks, one_block, 0)


def per_device(
    homolog_activations,
    homolog_tallies,
    standardize_gain,
    standardize_offset,
    former_factor_matrix,
    former_factor_offset,
    latter_factor_matrix,
    latter_factor_offset,
    pairwise_projection_matrix,
):
    depth, chain, features = homolog_activations.shape
    size_ri, size_rj, size_dp = (lax.axis_size(a) for a in ("ri", "rj", "dp"))
    split = size_rj * size_dp
    first_count, second_count = chain // size_ri, chain // split
    assert depth == 2 and first_count == TILE and second_count % TILE == 0 and chain % LANES == 0
    left_unit, right_unit = ROWS, ROWS * (second_count // TILE)
    total = size_ri * split
    bits = []
    bit = total // 2
    while bit >= size_dp:
        bits.append(bit)
        bit //= 2
    core = size_dp // 2
    stages = [[bits[0] | core]] if len(bits) % 2 else []
    bits = bits[len(bits) % 2 :]
    for high, low in zip(bits[::2], bits[1::2]):
        stages.append([low | core, high | core, low | high])
    if core:
        stages.append([core])
    plan = Plan(stages, split, left_unit, right_unit)
    sent = [sum(count for _, _, count in message) for stage, _, message in plan.messages if stage == 0]

    vmem = pl.BlockSpec(memory_space=pltpu.VMEM)
    bf16, f32 = jnp.bfloat16, jnp.float32
    operands = (
        homolog_activations,
        homolog_tallies[None, :],
        standardize_gain[None, :],
        standardize_offset[None, :],
        former_factor_matrix.T,
        former_factor_offset[None, :],
        latter_factor_matrix.T,
        latter_factor_offset[None, :],
    )
    in_hbm = [pltpu.with_memory_space_constraint(a, pltpu.HBM) for a in operands + (pairwise_projection_matrix,)]
    *own, first_scale, second_scale, matrix = pl.pallas_call(
        functools.partial(panels_kernel, plan, split),
        out_shape=(
            *(jax.ShapeDtypeStruct((rows, LANES), bf16) for rows in [plan.rows] + sent),
            jax.ShapeDtypeStruct((first_count, LANES), f32),
            jax.ShapeDtypeStruct((second_count, LANES), f32),
            jax.ShapeDtypeStruct(pairwise_projection_matrix.shape, f32),
        ),
        in_specs=[pl.BlockSpec(memory_space=pltpu.HBM)] * len(in_hbm),
        out_specs=(vmem,) * (4 + len(sent)),
        scratch_shapes=[pltpu.VMEM(a.shape, a.dtype) for a in operands]
        + [
            pltpu.VMEM((chain // TILE * ROWS, LANES), bf16),
            pltpu.VMEM((chain // TILE * ROWS, LANES), bf16),
            pltpu.VMEM((chain, LANES), f32),
            pltpu.SemaphoreType.DMA((len(in_hbm),)),
        ],
        compiler_params=pltpu.CompilerParams(vmem_limit_bytes=VMEM_BYTES),
        name="panels",
    )(*in_hbm)

    axes = ("ri", "rj", "dp")
    swap = lambda v, m: lax.ppermute(v, axes, [(d, d ^ m) for d in range(total)])
    buffers = own[:1]
    stage_of = lambda s: [(mask, message) for stage, mask, message in plan.messages if stage == s]
    for s in range(len(stages)):
        if s == 0:
            messages = own[1:]
        else:
            messages = [jnp.concatenate([buffers[b][r : r + n] for b, r, n in m], 0) for _, m in stage_of(s)]
        buffers = buffers + [swap(v, mask) for v, (mask, _) in zip(messages, stage_of(s))]

    return pl.pallas_call(
        functools.partial(pairs_kernel, plan),
        out_shape=jax.ShapeDtypeStruct((first_count, second_count, LANES), f32),
        in_specs=[vmem] * (len(buffers) + 3),
        out_specs=pl.BlockSpec(memory_space=pl.ANY),
        scratch_shapes=[
            pltpu.VMEM((2 * total * ROWS, LANES), f32),
            pltpu.VMEM((2 * LANES, 4 * total * 2), bf16),
            pltpu.VMEM((first_count * TILE, 8 * LANES), bf16),
            pltpu.VMEM((8 * LANES, 2 * LANES), bf16),
            pltpu.VMEM((4, first_count * 8, LANES), f32),
            pltpu.SemaphoreType.DMA((4,)),
        ],
        compiler_params=pltpu.CompilerParams(vmem_limit_bytes=VMEM_BYTES),
        name="pairs",
    )(*buffers, matrix, first_scale, second_scale)


def solution(mesh):
    placed = (P(("grp", "ri", "rj", "dp"), None, None), P("grp"), P(), P(), P(), P(), P(), P(), P())
    return jax.shard_map(
        per_device,
        mesh=mesh,
        in_specs=placed,
        out_specs=P(("grp", "ri"), ("rj", "dp"), None),
        check_vma=False,
    )
```

```python
import functools

import jax
import jax.numpy as jnp
from jax import lax
from jax.experimental import pallas as pl
from jax.experimental.pallas import tpu as pltpu
from jax.sharding import PartitionSpec as P

LANES = 128
TILE = 32
ROWS = 16
VMEM_BYTES = 32 * 1024 * 1024


def distinct(values):
    return sorted(set(values))


def reach(stages):
    found = [0]
    for masks in stages:
        found = [f ^ m for m in [0] + masks for f in found]
    return found


class Plan:
    def __init__(self, stages, split, left_unit, right_unit):
        firsts = lambda s: distinct(m // split for m in reach(s))
        seconds = lambda s: distinct(m % split for m in reach(s))
        left, right, self.own, self.rows = {}, {}, [], 0
        for kind, held, positions, unit in (
            ("L", left, firsts(stages), left_unit),
            ("R", right, seconds(stages), right_unit),
        ):
            for p in positions:
                held[p] = [(0, self.rows)]
                self.own.append((kind, p))
                self.rows += unit
        self.messages, buffer = [], 0
        for stage, masks in enumerate(stages):
            rest = stages[stage + 1 :]
            new_left = {p: list(left[p]) for p in firsts(rest)}
            new_right = {p: list(right[p]) for p in seconds(rest)}
            for mask in masks:
                buffer += 1
                message, at = [], 0
                for new, old, shift, unit in (
                    (new_left, left, mask // split, left_unit),
                    (new_right, right, mask % split, right_unit),
                ):
                    for p in new:
                        for source, row in old[p ^ shift]:
                            if message and message[-1][0] == source and sum(message[-1][1:]) == row:
                                message[-1] = (source, message[-1][1], message[-1][2] + unit)
                            else:
                                message.append((source, row, unit))
                            new[p].append((buffer, at))
                            at += unit
                self.messages.append((stage, mask, message))
            left, right = new_left, new_right
        self.buffers = buffer + 1
        self.left, self.right = left[0], right[0]


def panels_kernel(
    plan, split, x_hbm, tallies_hbm, gain_hbm, offset_hbm, former_hbm, former_bias_hbm, latter_hbm, latter_bias_hbm,
    matrix_hbm, *refs,
):
    sends = sum(stage == 0 for stage, _, _ in plan.messages)
    own_ref, *send_refs = refs[: 1 + sends]
    first_ref, second_ref, matrix_ref = refs[1 + sends : 4 + sends]
    x_ref, tallies_ref, gain_ref, offset_ref, former_ref, former_bias_ref, latter_ref, latter_bias_ref = refs[4 + sends : 12 + sends]
    left_ref, right_ref, down_ref, sems = refs[12 + sends :]
    depth, chain, features = x_ref.shape
    width = former_ref.shape[0]
    first = lax.axis_index("ri")
    second = lax.axis_index("rj") * lax.axis_size("dp") + lax.axis_index("dp")
    row_start = (first * split + second) * depth

    sources = (x_hbm, latter_hbm, former_hbm, gain_hbm, offset_hbm, tallies_hbm, latter_bias_hbm, former_bias_hbm)
    targets = (x_ref, latter_ref, former_ref, gain_ref, offset_ref, tallies_ref, latter_bias_ref, former_bias_ref)
    copies_in = [pltpu.make_async_copy(a, b, sems.at[k]) for k, (a, b) in enumerate(zip(sources, targets))]
    matrix_copy = pltpu.make_async_copy(matrix_hbm, matrix_ref, sems.at[len(copies_in)])
    for copy in copies_in:
        copy.start()
    matrix_copy.start()
    for copy in copies_in:
        copy.wait()

    x = x_ref[...].reshape(depth * chain, features).astype(jnp.float32)
    center = x - jnp.mean(x, axis=-1, keepdims=True)
    spread = jnp.mean(center * center, axis=-1, keepdims=True)
    normed = center * lax.rsqrt(spread + 1e-05) * gain_ref[...] + offset_ref[...]
    normed = normed.astype(jnp.bfloat16)

    copies = LANES // width
    latter = latter_ref[...]
    former = former_ref[...]
    matrix = jnp.concatenate([latter] * copies + [former] * copies, axis=0)
    bias = jnp.concatenate([latter_bias_ref[...]] * copies + [former_bias_ref[...]] * copies, axis=1)
    both = lax.dot_general(normed, matrix, (((1,), (1,)), ((), ())), preferred_element_type=jnp.float32) + bias

    tallies = tallies_ref[...]
    lane_block = lax.broadcasted_iota(jnp.int32, (8, LANES), 1) // TILE
    for chunk in range(chain // LANES):
        lanes = slice(chunk * LANES, (chunk + 1) * LANES)
        across = jnp.broadcast_to(tallies[:, lanes], (LANES, LANES)).astype(jnp.float32)
        down = across.T
        down_ref[lanes] = down
        right_rows, left_rows = [], []
        for s in range(depth):
            row = (row_start + s).astype(jnp.float32)
            rows = slice(s * chain + chunk * LANES, s * chain + (chunk + 1) * LANES)
            right = both[rows, :LANES] * (row < down).astype(jnp.float32)
            left = both[rows, LANES:].T[:width] * (row < across[:width]).astype(jnp.float32)
            right_rows.append(right)
            left_rows.append(left)
        for b in range(LANES // TILE):
            tiles = []
            for s in range(depth):
                tile = None
                for q in range(copies):
                    part = right_rows[s][b * TILE + q * 8 : b * TILE + (q + 1) * 8]
                    tile = part if tile is None else jnp.where(lane_block == q, part, tile)
                tiles.append(tile)
            block = chunk * (LANES // TILE) + b
            right_ref[block * ROWS : (block + 1) * ROWS] = jnp.concatenate(tiles, 0).astype(jnp.bfloat16)
            tiles = []
            for s in range(depth):
                tile = None
                for q in range(copies):
                    part = left_rows[s][q * 8 : (q + 1) * 8]
                    shift = (q - b) * TILE % LANES
                    part = pltpu.roll(part, shift, 1) if shift else part
                    tile = part if tile is None else jnp.where(lane_block == q, part, tile)
                tiles.append(tile)
            left_ref[block * ROWS : (block + 1) * ROWS] = jnp.concatenate(tiles, 0).astype(jnp.bfloat16)

    right_unit = right_ref.shape[0] // split
    at = 0
    for kind, position in plan.own:
        source, index, unit = (left_ref, first, ROWS) if kind == "L" else (right_ref, second, right_unit)
        start = pl.multiple_of((index ^ position) * unit, ROWS)
        own_ref[at : at + unit] = source[pl.ds(start, unit)]
        at += unit
    for send_ref, (_, _, message) in zip(send_refs, plan.messages):
        at = 0
        for _, row, count in message:
            send_ref[at : at + count] = own_ref[row : row + count]
            at += count
    for out_ref, index in ((first_ref, first), (second_ref, second)):
        count = out_ref.shape[0]
        out_ref[...] = 1.0 / (down_ref[pl.ds(pl.multiple_of(index * count, TILE), count)] + 0.001)
    matrix_copy.wait()


def pairs_kernel(plan, *refs):
    buffers = refs[: plan.buffers]
    matrix_ref, first_ref, second_ref, out_ref = refs[plan.buffers : plan.buffers + 4]
    gather_ref, left_ref, outer_ref, wide_ref, done_ref, sems = refs[plan.buffers + 4 :]
    first_count, second_count, _ = out_ref.shape
    sources = len(plan.left)
    depth = sources * 2
    width = LANES // 4

    for k, (buffer, row) in enumerate(plan.left):
        gather_ref[k * ROWS : (k + 1) * ROWS] = buffers[buffer][row : row + ROWS].astype(jnp.float32)
    for half in range(2):
        stacked = jnp.concatenate([gather_ref[pl.ds(half * 4 + c, depth, stride=8)] for c in range(4)], 0)
        left_ref[half * LANES : (half + 1) * LANES] = stacked.T.astype(jnp.bfloat16)
    matrix = matrix_ref[...]
    high = matrix.astype(jnp.bfloat16)
    wide_ref[:, :LANES] = high
    wide_ref[:, LANES:] = (matrix - high.astype(jnp.float32)).astype(jnp.bfloat16)
    first_scale = first_ref[...]

    def one_block(block, carry):
        for k, (buffer, row) in enumerate(plan.right):
            start = pl.multiple_of(row + block * ROWS, ROWS)
            at = (sources + k) * ROWS
            gather_ref[at : at + ROWS] = buffers[buffer][pl.ds(start, ROWS)].astype(jnp.float32)
        left = left_ref[...]
        lane_block = lax.broadcasted_iota(jnp.int32, (depth, LANES), 1) // width
        zero = jnp.zeros((depth, LANES), jnp.bfloat16)
        turned = []
        for j8 in range(8):
            plain = gather_ref[pl.ds(sources * ROWS + j8, depth, stride=8)]
            turned.append([(pltpu.roll(plain, r * width, 1) if r else plain).astype(jnp.bfloat16) for r in range(4)])

        def outer(q):
            for j8 in range(0, 8, 2):
                spread = jnp.concatenate(
                    [
                        jnp.concatenate([jnp.where(lane_block == c, t[(c - q) % 4], zero) for c in range(4)], 0)
                        for t in turned[j8 : j8 + 2]
                    ],
                    1,
                )
                product = jnp.dot(left, spread, preferred_element_type=jnp.float32).astype(jnp.bfloat16)
                for at in range(2):
                    j = q * 8 + j8 + at
                    for half in range(2):
                        for gq in range(4):
                            rows = (half * 4 + gq) * TILE
                            group = gq * 2 + half
                            outer_ref[j * TILE : (j + 1) * TILE, group * LANES : (group + 1) * LANES] = (
                                product[rows : rows + TILE, at * LANES : (at + 1) * LANES]
                            )

        def project(q):
            rows = outer_ref[q * 8 * TILE : (q + 1) * 8 * TILE]
            projected = jnp.dot(rows, wide_ref[...], preferred_element_type=jnp.float32)
            projected = projected[:, :LANES] + projected[:, LANES:]
            start = pl.multiple_of(block * TILE + q * 8, 8)
            for k in range(8):
                scale = jnp.maximum(first_scale, second_ref[pl.ds(start + k, 1)])
                done_ref[q, pl.ds(k, first_count, stride=8)] = projected[k * TILE : (k + 1) * TILE] * scale
            return pltpu.make_async_copy(
                done_ref.at[q].reshape(first_count, 8, LANES), out_ref.at[:, pl.ds(start, 8)], sems.at[q]
            )

        outer(0)
        outer(1)
        copies = []
        for q in range(4):
            if q + 2 < 4:
                outer(q + 2)
            copies.append(project(q))
            copies[-1].start()
        for copy in copies:
            copy.wait()
        return carry

    blocks = second_count // TILE
    if blocks == 1:
        one_block(0, 0)
    else:
        lax.fori_loop(0, blocks, one_block, 0)


def per_device(
    homolog_activations,
    homolog_tallies,
    standardize_gain,
    standardize_offset,
    former_factor_matrix,
    former_factor_offset,
    latter_factor_matrix,
    latter_factor_offset,
    pairwise_projection_matrix,
):
    depth, chain, features = homolog_activations.shape
    size_ri, size_rj, size_dp = (lax.axis_size(a) for a in ("ri", "rj", "dp"))
    split = size_rj * size_dp
    first_count, second_count = chain // size_ri, chain // split
    assert depth == 2 and first_count == TILE and second_count % TILE == 0 and chain % LANES == 0
    left_unit, right_unit = ROWS, ROWS * (second_count // TILE)
    total = size_ri * split
    bits = []
    bit = total // 2
    while bit >= size_dp:
        bits.append(bit)
        bit //= 2
    core = size_dp // 2
    stages = [[bits[0] | core]] if len(bits) % 2 else []
    bits = bits[len(bits) % 2 :]
    for high, low in zip(bits[::2], bits[1::2]):
        stages.append([low | core, high | core, low | high | core])
    if core:
        stages.append([core])
    plan = Plan(stages, split, left_unit, right_unit)
    sent = [sum(count for _, _, count in message) for stage, _, message in plan.messages if stage == 0]

    vmem = pl.BlockSpec(memory_space=pltpu.VMEM)
    bf16, f32 = jnp.bfloat16, jnp.float32
    operands = (
        homolog_activations,
        homolog_tallies[None, :],
        standardize_gain[None, :],
        standardize_offset[None, :],
        former_factor_matrix.T,
        former_factor_offset[None, :],
        latter_factor_matrix.T,
        latter_factor_offset[None, :],
    )
    in_hbm = [pltpu.with_memory_space_constraint(a, pltpu.HBM) for a in operands + (pairwise_projection_matrix,)]
    *own, first_scale, second_scale, matrix = pl.pallas_call(
        functools.partial(panels_kernel, plan, split),
        out_shape=(
            *(jax.ShapeDtypeStruct((rows, LANES), bf16) for rows in [plan.rows] + sent),
            jax.ShapeDtypeStruct((first_count, LANES), f32),
            jax.ShapeDtypeStruct((second_count, LANES), f32),
            jax.ShapeDtypeStruct(pairwise_projection_matrix.shape, f32),
        ),
        in_specs=[pl.BlockSpec(memory_space=pltpu.HBM)] * len(in_hbm),
        out_specs=(vmem,) * (4 + len(sent)),
        scratch_shapes=[pltpu.VMEM(a.shape, a.dtype) for a in operands]
        + [
            pltpu.VMEM((chain // TILE * ROWS, LANES), bf16),
            pltpu.VMEM((chain // TILE * ROWS, LANES), bf16),
            pltpu.VMEM((chain, LANES), f32),
            pltpu.SemaphoreType.DMA((len(in_hbm),)),
        ],
        compiler_params=pltpu.CompilerParams(vmem_limit_bytes=VMEM_BYTES),
        name="panels",
    )(*in_hbm)

    axes = ("ri", "rj", "dp")
    me = lax.axis_index(axes)
    move = lambda v, mask_of: lax.ppermute(v, axes, [(d, d ^ mask_of(d)) for d in range(total)])
    buffers = own[:1]
    for s, masks in enumerate(stages):
        if s == 0:
            messages = own[1:]
        else:
            messages = [
                jnp.concatenate([buffers[b][r : r + n] for b, r, n in message], 0)
                for stage, _, message in plan.messages
                if stage == s
            ]
        if len(masks) == 3:
            one, two, across = masks
            low, high = one & ~core, two & ~core
            even = lambda d: ((d & low) != 0) == ((d & high) != 0)
            messages = [
                jnp.where(even(me), messages[1], messages[0]),
                jnp.where(even(me), messages[0], messages[1]),
                messages[2],
            ]
            messages = list(lax.optimization_barrier(tuple(messages)))
            ways = [lambda d: two if even(d) else one, lambda d: one if even(d) else two, lambda d: across]
        else:
            ways = [lambda d: masks[0]]
        buffers = buffers + [move(v, way) for v, way in zip(messages, ways)]

    return pl.pallas_call(
        functools.partial(pairs_kernel, plan),
        out_shape=jax.ShapeDtypeStruct((first_count, second_count, LANES), f32),
        in_specs=[vmem] * (len(buffers) + 3),
        out_specs=pl.BlockSpec(memory_space=pl.ANY),
        scratch_shapes=[
            pltpu.VMEM((2 * total * ROWS, LANES), f32),
            pltpu.VMEM((2 * LANES, 4 * total * 2), bf16),
            pltpu.VMEM((first_count * TILE, 8 * LANES), bf16),
            pltpu.VMEM((8 * LANES, 2 * LANES), bf16),
            pltpu.VMEM((4, first_count * 8, LANES), f32),
            pltpu.SemaphoreType.DMA((4,)),
        ],
        compiler_params=pltpu.CompilerParams(vmem_limit_bytes=VMEM_BYTES),
        name="pairs",
    )(*buffers, matrix, first_scale, second_scale)


def solution(mesh):
    placed = (P(("grp", "ri", "rj", "dp"), None, None), P("grp"), P(), P(), P(), P(), P(), P(), P())
    return jax.shard_map(
        per_device,
        mesh=mesh,
        in_specs=placed,
        out_specs=P(("grp", "ri"), ("rj", "dp"), None),
        check_vma=False,
    )
```

```python
import functools

import jax
import jax.numpy as jnp
from jax import lax
from jax.experimental import pallas as pl
from jax.experimental.pallas import tpu as pltpu
from jax.sharding import PartitionSpec as P

LANES = 128
TILE = 32
ROWS = 16
VMEM_BYTES = 32 * 1024 * 1024


def distinct(values):
    return sorted(set(values))


def reach(stages):
    found = [0]
    for masks in stages:
        found = [f ^ m for m in [0] + masks for f in found]
    return found


class Plan:
    def __init__(self, stages, split, left_unit, right_unit):
        firsts = lambda s: distinct(m // split for m in reach(s))
        seconds = lambda s: distinct(m % split for m in reach(s))
        left, right, self.own, self.rows = {}, {}, [], 0
        for kind, held, positions, unit in (
            ("L", left, firsts(stages), left_unit),
            ("R", right, seconds(stages), right_unit),
        ):
            for p in positions:
                held[p] = [(0, self.rows)]
                self.own.append((kind, p))
                self.rows += unit
        self.messages, buffer = [], 0
        for stage, masks in enumerate(stages):
            rest = stages[stage + 1 :]
            new_left = {p: list(left[p]) for p in firsts(rest)}
            new_right = {p: list(right[p]) for p in seconds(rest)}
            for mask in masks:
                buffer += 1
                message, at = [], 0
                for new, old, shift, unit in (
                    (new_left, left, mask // split, left_unit),
                    (new_right, right, mask % split, right_unit),
                ):
                    for p in new:
                        for source, row in old[p ^ shift]:
                            if message and message[-1][0] == source and sum(message[-1][1:]) == row:
                                message[-1] = (source, message[-1][1], message[-1][2] + unit)
                            else:
                                message.append((source, row, unit))
                            new[p].append((buffer, at))
                            at += unit
                self.messages.append((stage, mask, message))
            left, right = new_left, new_right
        self.buffers = buffer + 1
        self.left, self.right = left[0], right[0]


def panels_kernel(
    plan, split, x_hbm, tallies_hbm, gain_hbm, offset_hbm, former_hbm, former_bias_hbm, latter_hbm, latter_bias_hbm,
    matrix_hbm, *refs,
):
    sends = sum(stage == 0 for stage, _, _ in plan.messages)
    own_ref, *send_refs = refs[: 1 + sends]
    first_ref, second_ref, matrix_ref = refs[1 + sends : 4 + sends]
    x_ref, tallies_ref, gain_ref, offset_ref, former_ref, former_bias_ref, latter_ref, latter_bias_ref = refs[4 + sends : 12 + sends]
    left_ref, right_ref, down_ref, sems = refs[12 + sends :]
    depth, chain, features = x_ref.shape
    width = former_ref.shape[0]
    first = lax.axis_index("ri")
    second = lax.axis_index("rj") * lax.axis_size("dp") + lax.axis_index("dp")
    row_start = (first * split + second) * depth

    sources = (x_hbm, latter_hbm, former_hbm, gain_hbm, offset_hbm, tallies_hbm, latter_bias_hbm, former_bias_hbm)
    targets = (x_ref, latter_ref, former_ref, gain_ref, offset_ref, tallies_ref, latter_bias_ref, former_bias_ref)
    copies_in = [pltpu.make_async_copy(a, b, sems.at[k]) for k, (a, b) in enumerate(zip(sources, targets))]
    matrix_copy = pltpu.make_async_copy(matrix_hbm, matrix_ref, sems.at[len(copies_in)])
    for copy in copies_in:
        copy.start()
    matrix_copy.start()
    for copy in copies_in:
        copy.wait()

    x = x_ref[...].reshape(depth * chain, features).astype(jnp.float32)
    center = x - jnp.mean(x, axis=-1, keepdims=True)
    spread = jnp.mean(center * center, axis=-1, keepdims=True)
    normed = center * lax.rsqrt(spread + 1e-05) * gain_ref[...] + offset_ref[...]
    normed = normed.astype(jnp.bfloat16)

    copies = LANES // width
    latter = latter_ref[...]
    former = former_ref[...]
    matrix = jnp.concatenate([latter] * copies + [former] * copies, axis=0)
    bias = jnp.concatenate([latter_bias_ref[...]] * copies + [former_bias_ref[...]] * copies, axis=1)
    both = lax.dot_general(normed, matrix, (((1,), (1,)), ((), ())), preferred_element_type=jnp.float32) + bias

    tallies = tallies_ref[...]
    lane_block = lax.broadcasted_iota(jnp.int32, (8, LANES), 1) // TILE
    for chunk in range(chain // LANES):
        lanes = slice(chunk * LANES, (chunk + 1) * LANES)
        across = jnp.broadcast_to(tallies[:, lanes], (LANES, LANES)).astype(jnp.float32)
        down = across.T
        down_ref[lanes] = down
        right_rows, left_rows = [], []
        for s in range(depth):
            row = (row_start + s).astype(jnp.float32)
            rows = slice(s * chain + chunk * LANES, s * chain + (chunk + 1) * LANES)
            right = both[rows, :LANES] * (row < down).astype(jnp.float32)
            left = both[rows, LANES:].T[:width] * (row < across[:width]).astype(jnp.float32)
            right_rows.append(right)
            left_rows.append(left)
        for b in range(LANES // TILE):
            tiles = []
            for s in range(depth):
                tile = None
                for q in range(copies):
                    part = right_rows[s][b * TILE + q * 8 : b * TILE + (q + 1) * 8]
                    tile = part if tile is None else jnp.where(lane_block == q, part, tile)
                tiles.append(tile)
            block = chunk * (LANES // TILE) + b
            right_ref[block * ROWS : (block + 1) * ROWS] = jnp.concatenate(tiles, 0).astype(jnp.bfloat16)
            tiles = []
            for s in range(depth):
                tile = None
                for q in range(copies):
                    part = left_rows[s][q * 8 : (q + 1) * 8]
                    shift = (q - b) * TILE % LANES
                    part = pltpu.roll(part, shift, 1) if shift else part
                    tile = part if tile is None else jnp.where(lane_block == q, part, tile)
                tiles.append(tile)
            left_ref[block * ROWS : (block + 1) * ROWS] = jnp.concatenate(tiles, 0).astype(jnp.bfloat16)

    right_unit = right_ref.shape[0] // split
    at = 0
    for kind, position in plan.own:
        source, index, unit = (left_ref, first, ROWS) if kind == "L" else (right_ref, second, right_unit)
        start = pl.multiple_of((index ^ position) * unit, ROWS)
        own_ref[at : at + unit] = source[pl.ds(start, unit)]
        at += unit
    for send_ref, (_, _, message) in zip(send_refs, plan.messages):
        at = 0
        for _, row, count in message:
            send_ref[at : at + count] = own_ref[row : row + count]
            at += count
    for out_ref, index in ((first_ref, first), (second_ref, second)):
        count = out_ref.shape[0]
        out_ref[...] = 1.0 / (down_ref[pl.ds(pl.multiple_of(index * count, TILE), count)] + 0.001)
    matrix_copy.wait()


def gathered(scratch_ref, buffers, tiles, block):
    for k, (buffer, row) in enumerate(tiles):
        start = pl.multiple_of(row + block * ROWS, ROWS)
        scratch_ref[k * ROWS : (k + 1) * ROWS] = buffers[buffer][pl.ds(start, ROWS)].astype(jnp.float32)


def stacked(scratch_ref, half, depth):
    return jnp.concatenate([scratch_ref[pl.ds(half * 4 + c, depth, stride=8)] for c in range(4)], 0)


def turns(scratch_ref, j8, depth):
    plain = scratch_ref[pl.ds(j8, depth, stride=8)]
    return [(pltpu.roll(plain, r * LANES // 4, 1) if r else plain).astype(jnp.bfloat16) for r in range(4)]


def ready_kernel(plan, blocks, *refs):
    buffers = refs[: plan.buffers - 1]
    matrix_ref, wide_ref, stack_ref, turned_ref, gather_ref = refs[plan.buffers - 1 :]
    sources = len(plan.left) // 2
    depth = sources * 2
    gathered(gather_ref, buffers, plan.left[:sources], 0)
    for half in range(2):
        stack_ref[half] = stacked(gather_ref, half, depth)
    matrix = matrix_ref[...]
    high = matrix.astype(jnp.bfloat16)
    wide_ref[:, :LANES] = high
    wide_ref[:, LANES:] = (matrix - high.astype(jnp.float32)).astype(jnp.bfloat16)

    def one_block(block, carry):
        gathered(gather_ref, buffers, plan.right[:sources], block)
        for j8 in range(8):
            for r, value in enumerate(turns(gather_ref, j8, depth)):
                turned_ref[block, j8 * 4 + r] = value
        return carry

    if blocks == 1:
        one_block(0, 0)
    else:
        lax.fori_loop(0, blocks, one_block, 0)


def pairs_kernel(plan, *refs):
    last_ref, wide_ref, stack_ref, turned_ref, first_ref, second_ref, out_ref = refs[:7]
    gather_left_ref, gather_ref, left_ref, outer_ref, done_ref, sems = refs[7:]
    first_count, second_count, _ = out_ref.shape
    sources = len(plan.left) // 2
    depth = sources * 2
    width = LANES // 4
    buffers = {plan.buffers - 1: last_ref}

    gathered(gather_left_ref, buffers, plan.left[sources:], 0)
    for half in range(2):
        rows = jnp.concatenate([stack_ref[half], stacked(gather_left_ref, half, depth)], 0)
        left_ref[half * LANES : (half + 1) * LANES] = rows.T.astype(jnp.bfloat16)
    first_scale = first_ref[...]

    def one_block(block, carry):
        gathered(gather_ref, buffers, plan.right[sources:], block)
        left = left_ref[...]
        lane_block = lax.broadcasted_iota(jnp.int32, (depth, LANES), 1) // width
        zero = jnp.zeros((depth, LANES), jnp.bfloat16)
        turned = [
            ([turned_ref[block, j8 * 4 + r] for r in range(4)], turns(gather_ref, j8, depth)) for j8 in range(8)
        ]

        def outer(q):
            for j8 in range(0, 8, 2):
                spread = jnp.concatenate(
                    [
                        jnp.concatenate(
                            [jnp.where(lane_block == c, t[(c - q) % 4], zero) for t in both for c in range(4)], 0
                        )
                        for both in turned[j8 : j8 + 2]
                    ],
                    1,
                )
                product = jnp.dot(left, spread, preferred_element_type=jnp.float32).astype(jnp.bfloat16)
                for at in range(2):
                    j = q * 8 + j8 + at
                    for half in range(2):
                        for gq in range(4):
                            rows = (half * 4 + gq) * TILE
                            group = gq * 2 + half
                            outer_ref[j * TILE : (j + 1) * TILE, group * LANES : (group + 1) * LANES] = (
                                product[rows : rows + TILE, at * LANES : (at + 1) * LANES]
                            )

        def project(q):
            rows = outer_ref[q * 8 * TILE : (q + 1) * 8 * TILE]
            projected = jnp.dot(rows, wide_ref[...], preferred_element_type=jnp.float32)
            projected = projected[:, :LANES] + projected[:, LANES:]
            start = pl.multiple_of(block * TILE + q * 8, 8)
            for k in range(8):
                scale = jnp.maximum(first_scale, second_ref[pl.ds(start + k, 1)])
                done_ref[q, pl.ds(k, first_count, stride=8)] = projected[k * TILE : (k + 1) * TILE] * scale
            return pltpu.make_async_copy(
                done_ref.at[q].reshape(first_count, 8, LANES), out_ref.at[:, pl.ds(start, 8)], sems.at[q]
            )

        outer(0)
        outer(1)
        copies = []
        for q in range(4):
            if q + 2 < 4:
                outer(q + 2)
            copies.append(project(q))
            copies[-1].start()
        for copy in copies:
            copy.wait()
        return carry

    blocks = second_count // TILE
    if blocks == 1:
        one_block(0, 0)
    else:
        lax.fori_loop(0, blocks, one_block, 0)


def per_device(
    homolog_activations,
    homolog_tallies,
    standardize_gain,
    standardize_offset,
    former_factor_matrix,
    former_factor_offset,
    latter_factor_matrix,
    latter_factor_offset,
    pairwise_projection_matrix,
):
    depth, chain, features = homolog_activations.shape
    size_ri, size_rj, size_dp = (lax.axis_size(a) for a in ("ri", "rj", "dp"))
    split = size_rj * size_dp
    first_count, second_count = chain // size_ri, chain // split
    assert depth == 2 and first_count == TILE and second_count % TILE == 0 and chain % LANES == 0
    left_unit, right_unit = ROWS, ROWS * (second_count // TILE)
    total = size_ri * split
    bits = []
    bit = total // 2
    while bit >= size_dp:
        bits.append(bit)
        bit //= 2
    core = size_dp // 2
    stages = [[bits[0] | core]] if len(bits) % 2 else []
    bits = bits[len(bits) % 2 :]
    for high, low in zip(bits[::2], bits[1::2]):
        stages.append([low | core, high | core, low | high | core])
    if core:
        stages.append([core])
    plan = Plan(stages, split, left_unit, right_unit)
    sent = [sum(count for _, _, count in message) for stage, _, message in plan.messages if stage == 0]

    vmem = pl.BlockSpec(memory_space=pltpu.VMEM)
    bf16, f32 = jnp.bfloat16, jnp.float32
    operands = (
        homolog_activations,
        homolog_tallies[None, :],
        standardize_gain[None, :],
        standardize_offset[None, :],
        former_factor_matrix.T,
        former_factor_offset[None, :],
        latter_factor_matrix.T,
        latter_factor_offset[None, :],
    )
    in_hbm = [pltpu.with_memory_space_constraint(a, pltpu.HBM) for a in operands + (pairwise_projection_matrix,)]
    *own, first_scale, second_scale, matrix = pl.pallas_call(
        functools.partial(panels_kernel, plan, split),
        out_shape=(
            *(jax.ShapeDtypeStruct((rows, LANES), bf16) for rows in [plan.rows] + sent),
            jax.ShapeDtypeStruct((first_count, LANES), f32),
            jax.ShapeDtypeStruct((second_count, LANES), f32),
            jax.ShapeDtypeStruct(pairwise_projection_matrix.shape, f32),
        ),
        in_specs=[pl.BlockSpec(memory_space=pltpu.HBM)] * len(in_hbm),
        out_specs=(vmem,) * (4 + len(sent)),
        scratch_shapes=[pltpu.VMEM(a.shape, a.dtype) for a in operands]
        + [
            pltpu.VMEM((chain // TILE * ROWS, LANES), bf16),
            pltpu.VMEM((chain // TILE * ROWS, LANES), bf16),
            pltpu.VMEM((chain, LANES), f32),
            pltpu.SemaphoreType.DMA((len(in_hbm),)),
        ],
        compiler_params=pltpu.CompilerParams(vmem_limit_bytes=VMEM_BYTES),
        name="panels",
    )(*in_hbm)

    axes = ("ri", "rj", "dp")
    me = lax.axis_index(axes)
    move = lambda v, mask_of: lax.ppermute(v, axes, [(d, d ^ mask_of(d)) for d in range(total)])
    buffers = own[:1]
    for s, masks in enumerate(stages):
        if s == 0:
            messages = own[1:]
        else:
            messages = [
                jnp.concatenate([buffers[b][r : r + n] for b, r, n in message], 0)
                for stage, _, message in plan.messages
                if stage == s
            ]
        if len(masks) == 3:
            one, two, across = masks
            low, high = one & ~core, two & ~core
            even = lambda d: ((d & low) != 0) == ((d & high) != 0)
            messages = [
                jnp.where(even(me), messages[1], messages[0]),
                jnp.where(even(me), messages[0], messages[1]),
                messages[2],
            ]
            messages = list(lax.optimization_barrier(tuple(messages)))
            ways = [lambda d: two if even(d) else one, lambda d: one if even(d) else two, lambda d: across]
        else:
            ways = [lambda d: masks[0]]
        buffers = buffers + [move(v, way) for v, way in zip(messages, ways)]

    blocks, sources = second_count // TILE, total // 2
    wide, stack, turned = pl.pallas_call(
        functools.partial(ready_kernel, plan, blocks),
        out_shape=(
            jax.ShapeDtypeStruct((8 * LANES, 2 * LANES), bf16),
            jax.ShapeDtypeStruct((2, 8 * sources, LANES), f32),
            jax.ShapeDtypeStruct((blocks, 32, 2 * sources, LANES), bf16),
        ),
        in_specs=[vmem] * plan.buffers,
        out_specs=(vmem,) * 3,
        scratch_shapes=[pltpu.VMEM((sources * ROWS, LANES), f32)],
        compiler_params=pltpu.CompilerParams(vmem_limit_bytes=VMEM_BYTES),
        name="ready",
    )(*buffers[:-1], matrix)
    return pl.pallas_call(
        functools.partial(pairs_kernel, plan),
        out_shape=jax.ShapeDtypeStruct((first_count, second_count, LANES), f32),
        in_specs=[vmem] * 6,
        out_specs=pl.BlockSpec(memory_space=pl.ANY),
        scratch_shapes=[
            pltpu.VMEM((sources * ROWS, LANES), f32),
            pltpu.VMEM((sources * ROWS, LANES), f32),
            pltpu.VMEM((2 * LANES, 4 * total * 2), bf16),
            pltpu.VMEM((first_count * TILE, 8 * LANES), bf16),
            pltpu.VMEM((4, first_count * 8, LANES), f32),
            pltpu.SemaphoreType.DMA((4,)),
        ],
        compiler_params=pltpu.CompilerParams(vmem_limit_bytes=VMEM_BYTES),
        name="pairs",
    )(buffers[-1], wide, stack, turned, first_scale, second_scale)


def solution(mesh):
    placed = (P(("grp", "ri", "rj", "dp"), None, None), P("grp"), P(), P(), P(), P(), P(), P(), P())
    return jax.shard_map(
        per_device,
        mesh=mesh,
        in_specs=placed,
        out_specs=P(("grp", "ri"), ("rj", "dp"), None),
        check_vma=False,
    )
```

```python
import functools

import jax
import jax.numpy as jnp
from jax import lax
from jax.experimental import pallas as pl
from jax.experimental.pallas import tpu as pltpu
from jax.sharding import PartitionSpec as P

LANES = 128
TILE = 32
ROWS = 16
VMEM_BYTES = 32 * 1024 * 1024


def distinct(values):
    return sorted(set(values))


def reach(stages):
    found = [0]
    for masks in stages:
        found = [f ^ m for m in [0] + masks for f in found]
    return found


class Plan:
    def __init__(self, stages, split, left_unit, right_unit):
        firsts = lambda s: distinct(m // split for m in reach(s))
        seconds = lambda s: distinct(m % split for m in reach(s))
        left, right, self.own, self.rows = {}, {}, [], 0
        for kind, held, positions, unit in (
            ("L", left, firsts(stages), left_unit),
            ("R", right, seconds(stages), right_unit),
        ):
            for p in positions:
                held[p] = [(0, self.rows)]
                self.own.append((kind, p))
                self.rows += unit
        self.messages, buffer = [], 0
        for stage, masks in enumerate(stages):
            rest = stages[stage + 1 :]
            new_left = {p: list(left[p]) for p in firsts(rest)}
            new_right = {p: list(right[p]) for p in seconds(rest)}
            for mask in masks:
                buffer += 1
                message, at = [], 0
                for new, old, shift, unit in (
                    (new_left, left, mask // split, left_unit),
                    (new_right, right, mask % split, right_unit),
                ):
                    for p in new:
                        for source, row in old[p ^ shift]:
                            if message and message[-1][0] == source and sum(message[-1][1:]) == row:
                                message[-1] = (source, message[-1][1], message[-1][2] + unit)
                            else:
                                message.append((source, row, unit))
                            new[p].append((buffer, at))
                            at += unit
                self.messages.append((stage, mask, message))
            left, right = new_left, new_right
        self.buffers = buffer + 1
        self.left, self.right = left[0], right[0]


def panels_kernel(
    plan, split, x_hbm, tallies_hbm, gain_hbm, offset_hbm, former_hbm, former_bias_hbm, latter_hbm, latter_bias_hbm,
    matrix_hbm, *refs,
):
    sends = sum(stage == 0 for stage, _, _ in plan.messages)
    own_ref, *send_refs = refs[: 1 + sends]
    first_ref, second_ref, matrix_ref = refs[1 + sends : 4 + sends]
    x_ref, tallies_ref, gain_ref, offset_ref, former_ref, former_bias_ref, latter_ref, latter_bias_ref = refs[4 + sends : 12 + sends]
    left_ref, right_ref, down_ref, sems = refs[12 + sends :]
    depth, chain, features = x_ref.shape
    width = former_ref.shape[0]
    first = lax.axis_index("ri")
    second = lax.axis_index("rj") * lax.axis_size("dp") + lax.axis_index("dp")
    row_start = (first * split + second) * depth

    sources = (x_hbm, latter_hbm, former_hbm, gain_hbm, offset_hbm, tallies_hbm, latter_bias_hbm, former_bias_hbm)
    targets = (x_ref, latter_ref, former_ref, gain_ref, offset_ref, tallies_ref, latter_bias_ref, former_bias_ref)
    copies_in = [pltpu.make_async_copy(a, b, sems.at[k]) for k, (a, b) in enumerate(zip(sources, targets))]
    matrix_copy = pltpu.make_async_copy(matrix_hbm, matrix_ref, sems.at[len(copies_in)])
    for copy in copies_in:
        copy.start()
    matrix_copy.start()
    for copy in copies_in:
        copy.wait()

    x = x_ref[...].reshape(depth * chain, features).astype(jnp.float32)
    center = x - jnp.mean(x, axis=-1, keepdims=True)
    spread = jnp.mean(center * center, axis=-1, keepdims=True)
    normed = center * lax.rsqrt(spread + 1e-05) * gain_ref[...] + offset_ref[...]
    normed = normed.astype(jnp.bfloat16)

    copies = LANES // width
    latter = latter_ref[...]
    former = former_ref[...]
    matrix = jnp.concatenate([latter] * copies + [former] * copies, axis=0)
    bias = jnp.concatenate([latter_bias_ref[...]] * copies + [former_bias_ref[...]] * copies, axis=1)
    both = lax.dot_general(normed, matrix, (((1,), (1,)), ((), ())), preferred_element_type=jnp.float32) + bias

    tallies = tallies_ref[...]
    lane_block = lax.broadcasted_iota(jnp.int32, (8, LANES), 1) // TILE
    for chunk in range(chain // LANES):
        lanes = slice(chunk * LANES, (chunk + 1) * LANES)
        across = jnp.broadcast_to(tallies[:, lanes], (LANES, LANES)).astype(jnp.float32)
        down = across.T
        down_ref[lanes] = down
        right_rows, left_rows = [], []
        for s in range(depth):
            row = (row_start + s).astype(jnp.float32)
            rows = slice(s * chain + chunk * LANES, s * chain + (chunk + 1) * LANES)
            right = both[rows, :LANES] * (row < down).astype(jnp.float32)
            left = both[rows, LANES:].T[:width] * (row < across[:width]).astype(jnp.float32)
            right_rows.append(right)
            left_rows.append(left)
        for b in range(LANES // TILE):
            tiles = []
            for s in range(depth):
                tile = None
                for q in range(copies):
                    part = right_rows[s][b * TILE + q * 8 : b * TILE + (q + 1) * 8]
                    tile = part if tile is None else jnp.where(lane_block == q, part, tile)
                tiles.append(tile)
            block = chunk * (LANES // TILE) + b
            right_ref[block * ROWS : (block + 1) * ROWS] = jnp.concatenate(tiles, 0).astype(jnp.bfloat16)
            tiles = []
            for s in range(depth):
                tile = None
                for q in range(copies):
                    part = left_rows[s][q * 8 : (q + 1) * 8]
                    shift = (q - b) * TILE % LANES
                    part = pltpu.roll(part, shift, 1) if shift else part
                    tile = part if tile is None else jnp.where(lane_block == q, part, tile)
                tiles.append(tile)
            left_ref[block * ROWS : (block + 1) * ROWS] = jnp.concatenate(tiles, 0).astype(jnp.bfloat16)

    right_unit = right_ref.shape[0] // split
    at = 0
    for kind, position in plan.own:
        source, index, unit = (left_ref, first, ROWS) if kind == "L" else (right_ref, second, right_unit)
        start = pl.multiple_of((index ^ position) * unit, ROWS)
        own_ref[at : at + unit] = source[pl.ds(start, unit)]
        at += unit
    for send_ref, (_, _, message) in zip(send_refs, plan.messages):
        at = 0
        for _, row, count in message:
            send_ref[at : at + count] = own_ref[row : row + count]
            at += count
    for out_ref, index in ((first_ref, first), (second_ref, second)):
        count = out_ref.shape[0]
        out_ref[...] = 1.0 / (down_ref[pl.ds(pl.multiple_of(index * count, TILE), count)] + 0.001)
    matrix_copy.wait()


def gathered(scratch_ref, buffers, tiles, block):
    for k, (buffer, row) in enumerate(tiles):
        start = pl.multiple_of(row + block * ROWS, ROWS)
        scratch_ref[k * ROWS : (k + 1) * ROWS] = buffers[buffer][pl.ds(start, ROWS)].astype(jnp.float32)


def stacked(scratch_ref, half, depth):
    return jnp.concatenate([scratch_ref[pl.ds(half * 4 + c, depth, stride=8)] for c in range(4)], 0)


def turns(scratch_ref, j8, depth):
    plain = scratch_ref[pl.ds(j8, depth, stride=8)]
    return [(pltpu.roll(plain, r * LANES // 4, 1) if r else plain).astype(jnp.bfloat16) for r in range(4)]


def ready_kernel(plan, blocks, *refs):
    buffers = refs[: plan.buffers - 1]
    matrix_ref, wide_ref, stack_ref, turned_ref, gather_ref = refs[plan.buffers - 1 :]
    sources = len(plan.left) // 2
    depth = sources * 2
    gathered(gather_ref, buffers, plan.left[:sources], 0)
    for half in range(2):
        stack_ref[half] = stacked(gather_ref, half, depth)
    matrix = matrix_ref[...]
    high = matrix.astype(jnp.bfloat16)
    wide_ref[:, :LANES] = high
    wide_ref[:, LANES:] = (matrix - high.astype(jnp.float32)).astype(jnp.bfloat16)

    def one_block(block, carry):
        gathered(gather_ref, buffers, plan.right[:sources], block)
        for j8 in range(8):
            for r, value in enumerate(turns(gather_ref, j8, depth)):
                turned_ref[block, j8 * 4 + r] = value
        return carry

    if blocks == 1:
        one_block(0, 0)
    else:
        lax.fori_loop(0, blocks, one_block, 0)


def pairs_kernel(plan, *refs):
    last_ref, wide_ref, stack_ref, turned_ref, first_ref, second_ref, out_ref = refs[:7]
    gather_left_ref, gather_ref, left_ref, outer_ref, done_ref, sems = refs[7:]
    first_count, second_count, _ = out_ref.shape
    sources = len(plan.left) // 2
    depth = sources * 2
    width = LANES // 4
    buffers = {plan.buffers - 1: last_ref}

    gathered(gather_left_ref, buffers, plan.left[sources:], 0)
    for half in range(2):
        rows = jnp.concatenate([stack_ref[half], stacked(gather_left_ref, half, depth)], 0)
        left_ref[half * LANES : (half + 1) * LANES] = rows.T.astype(jnp.bfloat16)
    first_scale = first_ref[...]

    def one_block(block, carry):
        gathered(gather_ref, buffers, plan.right[sources:], block)
        left = left_ref[...]
        lane_block = lax.broadcasted_iota(jnp.int32, (depth, LANES), 1) // width
        zero = jnp.zeros((depth, LANES), jnp.bfloat16)
        turned = [
            ([turned_ref[block, j8 * 4 + r] for r in range(4)], turns(gather_ref, j8, depth)) for j8 in range(8)
        ]

        def outer(q):
            for j8 in range(0, 8, 2):
                spread = jnp.concatenate(
                    [
                        jnp.concatenate(
                            [jnp.where(lane_block == c, t[(c - q) % 4], zero) for t in both for c in range(4)], 0
                        )
                        for both in turned[j8 : j8 + 2]
                    ],
                    1,
                )
                product = jnp.dot(left, spread, preferred_element_type=jnp.float32).astype(jnp.bfloat16)
                for at in range(2):
                    j = q * 8 + j8 + at
                    for half in range(2):
                        for gq in range(4):
                            rows = (half * 4 + gq) * TILE
                            group = gq * 2 + half
                            outer_ref[j * TILE : (j + 1) * TILE, group * LANES : (group + 1) * LANES] = (
                                product[rows : rows + TILE, at * LANES : (at + 1) * LANES]
                            )

        def project(q):
            rows = outer_ref[q * 8 * TILE : (q + 1) * 8 * TILE]
            projected = jnp.dot(rows, wide_ref[...], preferred_element_type=jnp.float32)
            projected = projected[:, :LANES] + projected[:, LANES:]
            start = pl.multiple_of(block * TILE + q * 8, 8)
            for k in range(8):
                scale = jnp.maximum(first_scale, second_ref[pl.ds(start + k, 1)])
                done_ref[q, pl.ds(k, first_count, stride=8)] = projected[k * TILE : (k + 1) * TILE] * scale
            return pltpu.make_async_copy(
                done_ref.at[q].reshape(first_count, 8, LANES), out_ref.at[:, pl.ds(start, 8)], sems.at[q]
            )

        outer(0)
        outer(1)
        copies = []
        for q in range(4):
            if q + 2 < 4:
                outer(q + 2)
            copies.append(project(q))
            copies[-1].start()
        for copy in copies:
            copy.wait()
        return carry

    blocks = second_count // TILE
    if blocks == 1:
        one_block(0, 0)
    else:
        lax.fori_loop(0, blocks, one_block, 0)


def per_device(
    homolog_activations,
    homolog_tallies,
    standardize_gain,
    standardize_offset,
    former_factor_matrix,
    former_factor_offset,
    latter_factor_matrix,
    latter_factor_offset,
    pairwise_projection_matrix,
):
    depth, chain, features = homolog_activations.shape
    size_ri, size_rj, size_dp = (lax.axis_size(a) for a in ("ri", "rj", "dp"))
    split = size_rj * size_dp
    first_count, second_count = chain // size_ri, chain // split
    assert depth == 2 and first_count == TILE and second_count % TILE == 0 and chain % LANES == 0
    left_unit, right_unit = ROWS, ROWS * (second_count // TILE)
    total = size_ri * split
    bits = []
    bit = total // 2
    while bit >= size_dp:
        bits.append(bit)
        bit //= 2
    core = size_dp // 2
    stages = [[bits[0] | core]] if len(bits) % 2 else []
    bits = bits[len(bits) % 2 :]
    for high, low in zip(bits[::2], bits[1::2]):
        stages.append([low | core, high | core, low | high | core])
    if core:
        stages.append([core])
    plan = Plan(stages, split, left_unit, right_unit)
    sent = [sum(count for _, _, count in message) for stage, _, message in plan.messages if stage == 0]

    vmem = pl.BlockSpec(memory_space=pltpu.VMEM)
    bf16, f32 = jnp.bfloat16, jnp.float32
    operands = (
        homolog_activations,
        homolog_tallies[None, :],
        standardize_gain[None, :],
        standardize_offset[None, :],
        former_factor_matrix.T,
        former_factor_offset[None, :],
        latter_factor_matrix.T,
        latter_factor_offset[None, :],
    )
    in_hbm = [pltpu.with_memory_space_constraint(a, pltpu.HBM) for a in operands + (pairwise_projection_matrix,)]
    *own, first_scale, second_scale, matrix = pl.pallas_call(
        functools.partial(panels_kernel, plan, split),
        out_shape=(
            *(jax.ShapeDtypeStruct((rows, LANES), bf16) for rows in [plan.rows] + sent),
            jax.ShapeDtypeStruct((first_count, LANES), f32),
            jax.ShapeDtypeStruct((second_count, LANES), f32),
            jax.ShapeDtypeStruct(pairwise_projection_matrix.shape, f32),
        ),
        in_specs=[pl.BlockSpec(memory_space=pltpu.HBM)] * len(in_hbm),
        out_specs=(vmem,) * (4 + len(sent)),
        scratch_shapes=[pltpu.VMEM(a.shape, a.dtype) for a in operands]
        + [
            pltpu.VMEM((chain // TILE * ROWS, LANES), bf16),
            pltpu.VMEM((chain // TILE * ROWS, LANES), bf16),
            pltpu.VMEM((chain, LANES), f32),
            pltpu.SemaphoreType.DMA((len(in_hbm),)),
        ],
        compiler_params=pltpu.CompilerParams(vmem_limit_bytes=VMEM_BYTES),
        name="panels",
    )(*in_hbm)

    axes = ("ri", "rj", "dp")
    me = lax.axis_index(axes)
    move = lambda v, mask_of: lax.ppermute(v, axes, [(d, d ^ mask_of(d)) for d in range(total)])
    buffers = own[:1]
    for s, masks in enumerate(stages):
        if s == 0:
            messages = own[1:]
        else:
            messages = [
                jnp.concatenate([buffers[b][r : r + n] for b, r, n in message], 0)
                for stage, _, message in plan.messages
                if stage == s
            ]
        if len(masks) == 3:
            one, two, across = masks
            high = two & ~core
            odd = lambda d: (d & high) != 0
            messages = [
                jnp.where(odd(me), messages[2], messages[1]),
                jnp.where(odd(me), messages[1], messages[2]),
                messages[0],
            ]
            messages = list(lax.optimization_barrier(tuple(messages)))
            ways = [lambda d: across if odd(d) else two, lambda d: two if odd(d) else across, lambda d: one]
        else:
            ways = [lambda d: masks[0]]
        buffers = buffers + [move(v, way) for v, way in zip(messages, ways)]

    blocks, sources = second_count // TILE, total // 2
    wide, stack, turned = pl.pallas_call(
        functools.partial(ready_kernel, plan, blocks),
        out_shape=(
            jax.ShapeDtypeStruct((8 * LANES, 2 * LANES), bf16),
            jax.ShapeDtypeStruct((2, 8 * sources, LANES), f32),
            jax.ShapeDtypeStruct((blocks, 32, 2 * sources, LANES), bf16),
        ),
        in_specs=[vmem] * plan.buffers,
        out_specs=(vmem,) * 3,
        scratch_shapes=[pltpu.VMEM((sources * ROWS, LANES), f32)],
        compiler_params=pltpu.CompilerParams(vmem_limit_bytes=VMEM_BYTES),
        name="ready",
    )(*buffers[:-1], matrix)
    return pl.pallas_call(
        functools.partial(pairs_kernel, plan),
        out_shape=jax.ShapeDtypeStruct((first_count, second_count, LANES), f32),
        in_specs=[vmem] * 6,
        out_specs=pl.BlockSpec(memory_space=pl.ANY),
        scratch_shapes=[
            pltpu.VMEM((sources * ROWS, LANES), f32),
            pltpu.VMEM((sources * ROWS, LANES), f32),
            pltpu.VMEM((2 * LANES, 4 * total * 2), bf16),
            pltpu.VMEM((first_count * TILE, 8 * LANES), bf16),
            pltpu.VMEM((4, first_count * 8, LANES), f32),
            pltpu.SemaphoreType.DMA((4,)),
        ],
        compiler_params=pltpu.CompilerParams(vmem_limit_bytes=VMEM_BYTES),
        name="pairs",
    )(buffers[-1], wide, stack, turned, first_scale, second_scale)


def solution(mesh):
    placed = (P(("grp", "ri", "rj", "dp"), None, None), P("grp"), P(), P(), P(), P(), P(), P(), P())
    return jax.shard_map(
        per_device,
        mesh=mesh,
        in_specs=placed,
        out_specs=P(("grp", "ri"), ("rj", "dp"), None),
        check_vma=False,
    )
```

```python
import functools

import jax
import jax.numpy as jnp
from jax import lax
from jax.experimental import pallas as pl
from jax.experimental.pallas import tpu as pltpu
from jax.sharding import PartitionSpec as P

LANES = 128
TILE = 32
ROWS = 16
VMEM_BYTES = 32 * 1024 * 1024


def distinct(values):
    return sorted(set(values))


def reach(stages):
    found = [0]
    for masks in stages:
        found = [f ^ m for m in [0] + masks for f in found]
    return found


class Plan:
    def __init__(self, stages, split, left_unit, right_unit):
        firsts = lambda s: distinct(m // split for m in reach(s))
        seconds = lambda s: distinct(m % split for m in reach(s))
        left, right, self.own, self.rows = {}, {}, [], 0
        for kind, held, positions, unit in (
            ("L", left, firsts(stages), left_unit),
            ("R", right, seconds(stages), right_unit),
        ):
            for p in positions:
                held[p] = [(0, self.rows)]
                self.own.append((kind, p))
                self.rows += unit
        self.messages, buffer = [], 0
        for stage, masks in enumerate(stages):
            rest = stages[stage + 1 :]
            new_left = {p: list(left[p]) for p in firsts(rest)}
            new_right = {p: list(right[p]) for p in seconds(rest)}
            for mask in masks:
                buffer += 1
                message, at = [], 0
                for new, old, shift, unit in (
                    (new_left, left, mask // split, left_unit),
                    (new_right, right, mask % split, right_unit),
                ):
                    for p in new:
                        for source, row in old[p ^ shift]:
                            if message and message[-1][0] == source and sum(message[-1][1:]) == row:
                                message[-1] = (source, message[-1][1], message[-1][2] + unit)
                            else:
                                message.append((source, row, unit))
                            new[p].append((buffer, at))
                            at += unit
                self.messages.append((stage, mask, message))
            left, right = new_left, new_right
        self.buffers = buffer + 1
        self.left, self.right = left[0], right[0]


def panels_kernel(
    plan, split, x_hbm, tallies_hbm, gain_hbm, offset_hbm, former_hbm, former_bias_hbm, latter_hbm, latter_bias_hbm,
    matrix_hbm, *refs,
):
    sends = sum(stage == 0 for stage, _, _ in plan.messages)
    own_ref, *send_refs = refs[: 1 + sends]
    first_ref, second_ref, matrix_ref = refs[1 + sends : 4 + sends]
    x_ref, tallies_ref, gain_ref, offset_ref, former_ref, former_bias_ref, latter_ref, latter_bias_ref = refs[4 + sends : 12 + sends]
    left_ref, right_ref, down_ref, sems = refs[12 + sends :]
    depth, chain, features = x_ref.shape
    width = former_ref.shape[0]
    first = lax.axis_index("ri")
    second = lax.axis_index("rj") * lax.axis_size("dp") + lax.axis_index("dp")
    row_start = (first * split + second) * depth

    sources = (x_hbm, latter_hbm, former_hbm, gain_hbm, offset_hbm, tallies_hbm, latter_bias_hbm, former_bias_hbm)
    targets = (x_ref, latter_ref, former_ref, gain_ref, offset_ref, tallies_ref, latter_bias_ref, former_bias_ref)
    copies_in = [pltpu.make_async_copy(a, b, sems.at[k]) for k, (a, b) in enumerate(zip(sources, targets))]
    matrix_copy = pltpu.make_async_copy(matrix_hbm, matrix_ref, sems.at[len(copies_in)])
    for copy in copies_in:
        copy.start()
    matrix_copy.start()
    x_copy, *others = copies_in
    for copy in others:
        copy.wait()
    copies = LANES // width
    matrix = jnp.concatenate([latter_ref[...]] * copies + [former_ref[...]] * copies, axis=0).T
    x_copy.wait()

    x = x_ref[...].reshape(depth * chain, features).astype(jnp.float32)
    center = x - jnp.mean(x, axis=-1, keepdims=True)
    spread = jnp.mean(center * center, axis=-1, keepdims=True)
    normed = center * lax.rsqrt(spread + 1e-05) * gain_ref[...] + offset_ref[...]
    normed = normed.astype(jnp.bfloat16)

    copies = LANES // width
    bias = jnp.concatenate([latter_bias_ref[...]] * copies + [former_bias_ref[...]] * copies, axis=1)
    both = lax.dot_general(normed, matrix, (((1,), (0,)), ((), ())), preferred_element_type=jnp.float32) + bias

    tallies = tallies_ref[...]
    lane_block = lax.broadcasted_iota(jnp.int32, (8, LANES), 1) // TILE
    for chunk in range(chain // LANES):
        lanes = slice(chunk * LANES, (chunk + 1) * LANES)
        across = jnp.broadcast_to(tallies[:, lanes], (LANES, LANES)).astype(jnp.float32)
        down = across.T
        down_ref[lanes] = down
        right_rows, left_rows = [], []
        for s in range(depth):
            row = (row_start + s).astype(jnp.float32)
            rows = slice(s * chain + chunk * LANES, s * chain + (chunk + 1) * LANES)
            right = both[rows, :LANES] * (row < down).astype(jnp.float32)
            left = both[rows, LANES:].T[:width] * (row < across[:width]).astype(jnp.float32)
            right_rows.append(right)
            left_rows.append(left)
        for b in range(LANES // TILE):
            tiles = []
            for s in range(depth):
                tile = None
                for q in range(copies):
                    part = right_rows[s][b * TILE + q * 8 : b * TILE + (q + 1) * 8]
                    tile = part if tile is None else jnp.where(lane_block == q, part, tile)
                tiles.append(tile)
            block = chunk * (LANES // TILE) + b
            right_ref[block * ROWS : (block + 1) * ROWS] = jnp.concatenate(tiles, 0).astype(jnp.bfloat16)
            tiles = []
            for s in range(depth):
                tile = None
                for q in range(copies):
                    part = left_rows[s][q * 8 : (q + 1) * 8]
                    shift = (q - b) * TILE % LANES
                    part = pltpu.roll(part, shift, 1) if shift else part
                    tile = part if tile is None else jnp.where(lane_block == q, part, tile)
                tiles.append(tile)
            left_ref[block * ROWS : (block + 1) * ROWS] = jnp.concatenate(tiles, 0).astype(jnp.bfloat16)

    right_unit = right_ref.shape[0] // split
    at = 0
    for kind, position in plan.own:
        source, index, unit = (left_ref, first, ROWS) if kind == "L" else (right_ref, second, right_unit)
        start = pl.multiple_of((index ^ position) * unit, ROWS)
        own_ref[at : at + unit] = source[pl.ds(start, unit)]
        at += unit
    for send_ref, (_, _, message) in zip(send_refs, plan.messages):
        at = 0
        for _, row, count in message:
            send_ref[at : at + count] = own_ref[row : row + count]
            at += count
    for out_ref, index in ((first_ref, first), (second_ref, second)):
        count = out_ref.shape[0]
        out_ref[...] = 1.0 / (down_ref[pl.ds(pl.multiple_of(index * count, TILE), count)] + 0.001)
    matrix_copy.wait()


def gathered(scratch_ref, buffers, tiles, block):
    for k, (buffer, row) in enumerate(tiles):
        start = pl.multiple_of(row + block * ROWS, ROWS)
        scratch_ref[k * ROWS : (k + 1) * ROWS] = buffers[buffer][pl.ds(start, ROWS)].astype(jnp.float32)


def stacked(scratch_ref, half, depth):
    return jnp.concatenate([scratch_ref[pl.ds(half * 4 + c, depth, stride=8)] for c in range(4)], 0)


def turns(scratch_ref, j8, depth):
    plain = scratch_ref[pl.ds(j8, depth, stride=8)]
    return [(pltpu.roll(plain, r * LANES // 4, 1) if r else plain).astype(jnp.bfloat16) for r in range(4)]


def ready_kernel(plan, blocks, *refs):
    buffers = refs[: plan.buffers - 1]
    matrix_ref, wide_ref, stack_ref, turned_ref, gather_ref = refs[plan.buffers - 1 :]
    sources = len(plan.left) // 2
    depth = sources * 2
    gathered(gather_ref, buffers, plan.left[:sources], 0)
    for half in range(2):
        stack_ref[half] = stacked(gather_ref, half, depth)
    matrix = matrix_ref[...]
    high = matrix.astype(jnp.bfloat16)
    wide_ref[:, :LANES] = high
    wide_ref[:, LANES:] = (matrix - high.astype(jnp.float32)).astype(jnp.bfloat16)

    def one_block(block, carry):
        gathered(gather_ref, buffers, plan.right[:sources], block)
        for j8 in range(8):
            for r, value in enumerate(turns(gather_ref, j8, depth)):
                turned_ref[block, j8 * 4 + r] = value
        return carry

    if blocks == 1:
        one_block(0, 0)
    else:
        lax.fori_loop(0, blocks, one_block, 0)


def pairs_kernel(plan, *refs):
    last_ref, wide_ref, stack_ref, turned_ref, first_ref, second_ref, out_ref = refs[:7]
    gather_left_ref, gather_ref, left_ref, outer_ref, done_ref, sems = refs[7:]
    first_count, second_count, _ = out_ref.shape
    sources = len(plan.left) // 2
    depth = sources * 2
    width = LANES // 4
    buffers = {plan.buffers - 1: last_ref}

    gathered(gather_left_ref, buffers, plan.left[sources:], 0)
    for half in range(2):
        rows = jnp.concatenate([stack_ref[half], stacked(gather_left_ref, half, depth)], 0)
        left_ref[half * LANES : (half + 1) * LANES] = rows.T.astype(jnp.bfloat16)
    first_scale = first_ref[...]

    def one_block(block, carry):
        gathered(gather_ref, buffers, plan.right[sources:], block)
        left = left_ref[...]
        lane_block = lax.broadcasted_iota(jnp.int32, (depth, LANES), 1) // width
        zero = jnp.zeros((depth, LANES), jnp.bfloat16)
        turned = [
            ([turned_ref[block, j8 * 4 + r] for r in range(4)], turns(gather_ref, j8, depth)) for j8 in range(8)
        ]

        def outer(q):
            for j8 in range(0, 8, 2):
                spread = jnp.concatenate(
                    [
                        jnp.concatenate(
                            [jnp.where(lane_block == c, t[(c - q) % 4], zero) for t in both for c in range(4)], 0
                        )
                        for both in turned[j8 : j8 + 2]
                    ],
                    1,
                )
                product = jnp.dot(left, spread, preferred_element_type=jnp.float32).astype(jnp.bfloat16)
                for at in range(2):
                    j = q * 8 + j8 + at
                    for half in range(2):
                        for gq in range(4):
                            rows = (half * 4 + gq) * TILE
                            group = gq * 2 + half
                            outer_ref[j * TILE : (j + 1) * TILE, group * LANES : (group + 1) * LANES] = (
                                product[rows : rows + TILE, at * LANES : (at + 1) * LANES]
                            )

        def project(q):
            rows = outer_ref[q * 8 * TILE : (q + 1) * 8 * TILE]
            projected = jnp.dot(rows, wide_ref[...], preferred_element_type=jnp.float32)
            projected = projected[:, :LANES] + projected[:, LANES:]
            start = pl.multiple_of(block * TILE + q * 8, 8)
            for k in range(8):
                scale = jnp.maximum(first_scale, second_ref[pl.ds(start + k, 1)])
                done_ref[q, pl.ds(k, first_count, stride=8)] = projected[k * TILE : (k + 1) * TILE] * scale
            return pltpu.make_async_copy(
                done_ref.at[q].reshape(first_count, 8, LANES), out_ref.at[:, pl.ds(start, 8)], sems.at[q]
            )

        outer(0)
        outer(1)
        copies = []
        for q in range(4):
            if q + 2 < 4:
                outer(q + 2)
            copies.append(project(q))
            copies[-1].start()
        for copy in copies:
            copy.wait()
        return carry

    blocks = second_count // TILE
    if blocks == 1:
        one_block(0, 0)
    else:
        lax.fori_loop(0, blocks, one_block, 0)


def per_device(
    homolog_activations,
    homolog_tallies,
    standardize_gain,
    standardize_offset,
    former_factor_matrix,
    former_factor_offset,
    latter_factor_matrix,
    latter_factor_offset,
    pairwise_projection_matrix,
):
    depth, chain, features = homolog_activations.shape
    size_ri, size_rj, size_dp = (lax.axis_size(a) for a in ("ri", "rj", "dp"))
    split = size_rj * size_dp
    first_count, second_count = chain // size_ri, chain // split
    assert depth == 2 and first_count == TILE and second_count % TILE == 0 and chain % LANES == 0
    left_unit, right_unit = ROWS, ROWS * (second_count // TILE)
    total = size_ri * split
    bits = []
    bit = total // 2
    while bit >= size_dp:
        bits.append(bit)
        bit //= 2
    core = size_dp // 2
    stages = [[bits[0] | core]] if len(bits) % 2 else []
    bits = bits[len(bits) % 2 :]
    for high, low in zip(bits[::2], bits[1::2]):
        stages.append([low | core, high | core, low | high | core])
    if core:
        stages.append([core])
    plan = Plan(stages, split, left_unit, right_unit)
    sent = [sum(count for _, _, count in message) for stage, _, message in plan.messages if stage == 0]

    vmem = pl.BlockSpec(memory_space=pltpu.VMEM)
    bf16, f32 = jnp.bfloat16, jnp.float32
    operands = (
        homolog_activations,
        homolog_tallies[None, :],
        standardize_gain[None, :],
        standardize_offset[None, :],
        former_factor_matrix.T,
        former_factor_offset[None, :],
        latter_factor_matrix.T,
        latter_factor_offset[None, :],
    )
    in_hbm = [pltpu.with_memory_space_constraint(a, pltpu.HBM) for a in operands + (pairwise_projection_matrix,)]
    *own, first_scale, second_scale, matrix = pl.pallas_call(
        functools.partial(panels_kernel, plan, split),
        out_shape=(
            *(jax.ShapeDtypeStruct((rows, LANES), bf16) for rows in [plan.rows] + sent),
            jax.ShapeDtypeStruct((first_count, LANES), f32),
            jax.ShapeDtypeStruct((second_count, LANES), f32),
            jax.ShapeDtypeStruct(pairwise_projection_matrix.shape, f32),
        ),
        in_specs=[pl.BlockSpec(memory_space=pltpu.HBM)] * len(in_hbm),
        out_specs=(vmem,) * (4 + len(sent)),
        scratch_shapes=[pltpu.VMEM(a.shape, a.dtype) for a in operands]
        + [
            pltpu.VMEM((chain // TILE * ROWS, LANES), bf16),
            pltpu.VMEM((chain // TILE * ROWS, LANES), bf16),
            pltpu.VMEM((chain, LANES), f32),
            pltpu.SemaphoreType.DMA((len(in_hbm),)),
        ],
        compiler_params=pltpu.CompilerParams(vmem_limit_bytes=VMEM_BYTES),
        name="panels",
    )(*in_hbm)

    axes = ("ri", "rj", "dp")
    me = lax.axis_index(axes)
    move = lambda v, mask_of: lax.ppermute(v, axes, [(d, d ^ mask_of(d)) for d in range(total)])
    buffers = own[:1]
    for s, masks in enumerate(stages):
        if s == 0:
            messages = own[1:]
        else:
            messages = [
                jnp.concatenate([buffers[b][r : r + n] for b, r, n in message], 0)
                for stage, _, message in plan.messages
                if stage == s
            ]
        if len(masks) == 3:
            one, two, across = masks
            low, high = one & ~core, two & ~core
            even = lambda d: ((d & low) != 0) == ((d & high) != 0)
            messages = [
                jnp.where(even(me), messages[1], messages[0]),
                jnp.where(even(me), messages[0], messages[1]),
                messages[2],
            ]
            messages = list(lax.optimization_barrier(tuple(messages)))
            ways = [lambda d: two if even(d) else one, lambda d: one if even(d) else two, lambda d: across]
        else:
            ways = [lambda d: masks[0]]
        buffers = buffers + [move(v, way) for v, way in zip(messages, ways)]

    blocks, sources = second_count // TILE, total // 2
    wide, stack, turned = pl.pallas_call(
        functools.partial(ready_kernel, plan, blocks),
        out_shape=(
            jax.ShapeDtypeStruct((8 * LANES, 2 * LANES), bf16),
            jax.ShapeDtypeStruct((2, 8 * sources, LANES), f32),
            jax.ShapeDtypeStruct((blocks, 32, 2 * sources, LANES), bf16),
        ),
        in_specs=[vmem] * plan.buffers,
        out_specs=(vmem,) * 3,
        scratch_shapes=[pltpu.VMEM((sources * ROWS, LANES), f32)],
        compiler_params=pltpu.CompilerParams(vmem_limit_bytes=VMEM_BYTES),
        name="ready",
    )(*buffers[:-1], matrix)
    return pl.pallas_call(
        functools.partial(pairs_kernel, plan),
        out_shape=jax.ShapeDtypeStruct((first_count, second_count, LANES), f32),
        in_specs=[vmem] * 6,
        out_specs=pl.BlockSpec(memory_space=pl.ANY),
        scratch_shapes=[
            pltpu.VMEM((sources * ROWS, LANES), f32),
            pltpu.VMEM((sources * ROWS, LANES), f32),
            pltpu.VMEM((2 * LANES, 4 * total * 2), bf16),
            pltpu.VMEM((first_count * TILE, 8 * LANES), bf16),
            pltpu.VMEM((4, first_count * 8, LANES), f32),
            pltpu.SemaphoreType.DMA((4,)),
        ],
        compiler_params=pltpu.CompilerParams(vmem_limit_bytes=VMEM_BYTES),
        name="pairs",
    )(buffers[-1], wide, stack, turned, first_scale, second_scale)


def solution(mesh):
    placed = (P(("grp", "ri", "rj", "dp"), None, None), P("grp"), P(), P(), P(), P(), P(), P(), P())
    return jax.shard_map(
        per_device,
        mesh=mesh,
        in_specs=placed,
        out_specs=P(("grp", "ri"), ("rj", "dp"), None),
        check_vma=False,
    )
```

```python
import functools

import jax
import jax.numpy as jnp
from jax import lax
from jax.experimental import pallas as pl
from jax.experimental.pallas import tpu as pltpu
from jax.sharding import PartitionSpec as P

LANES = 128
TILE = 32
ROWS = 16
VMEM_BYTES = 32 * 1024 * 1024


def distinct(values):
    return sorted(set(values))


def reach(stages):
    found = [0]
    for masks in stages:
        found = [f ^ m for m in [0] + masks for f in found]
    return found


class Plan:
    def __init__(self, stages, split, left_unit, right_unit):
        firsts = lambda s: distinct(m // split for m in reach(s))
        seconds = lambda s: distinct(m % split for m in reach(s))
        left, right, self.own, self.rows = {}, {}, [], 0
        for kind, held, positions, unit in (
            ("L", left, firsts(stages), left_unit),
            ("R", right, seconds(stages), right_unit),
        ):
            for p in positions:
                held[p] = [(0, self.rows)]
                self.own.append((kind, p))
                self.rows += unit
        self.messages, buffer = [], 0
        for stage, masks in enumerate(stages):
            rest = stages[stage + 1 :]
            new_left = {p: list(left[p]) for p in firsts(rest)}
            new_right = {p: list(right[p]) for p in seconds(rest)}
            for mask in masks:
                buffer += 1
                message, at = [], 0
                for new, old, shift, unit in (
                    (new_left, left, mask // split, left_unit),
                    (new_right, right, mask % split, right_unit),
                ):
                    for p in new:
                        for source, row in old[p ^ shift]:
                            if message and message[-1][0] == source and sum(message[-1][1:]) == row:
                                message[-1] = (source, message[-1][1], message[-1][2] + unit)
                            else:
                                message.append((source, row, unit))
                            new[p].append((buffer, at))
                            at += unit
                self.messages.append((stage, mask, message))
            left, right = new_left, new_right
        self.buffers = buffer + 1
        self.left, self.right = left[0], right[0]


def panels_kernel(
    plan, split, x_hbm, tallies_hbm, gain_hbm, offset_hbm, former_hbm, former_bias_hbm, latter_hbm, latter_bias_hbm,
    matrix_hbm, *refs,
):
    sends = sum(stage == 0 for stage, _, _ in plan.messages)
    own_ref, *send_refs = refs[: 1 + sends]
    first_ref, second_ref, matrix_ref = refs[1 + sends : 4 + sends]
    x_ref, tallies_ref, gain_ref, offset_ref, former_ref, former_bias_ref, latter_ref, latter_bias_ref = refs[4 + sends : 12 + sends]
    left_ref, right_ref, down_ref, sems = refs[12 + sends :]
    depth, chain, features = x_ref.shape
    width = former_ref.shape[0]
    first = lax.axis_index("ri")
    second = lax.axis_index("rj") * lax.axis_size("dp") + lax.axis_index("dp")
    row_start = (first * split + second) * depth

    sources = (x_hbm, latter_hbm, former_hbm, gain_hbm, offset_hbm, tallies_hbm, latter_bias_hbm, former_bias_hbm)
    targets = (x_ref, latter_ref, former_ref, gain_ref, offset_ref, tallies_ref, latter_bias_ref, former_bias_ref)
    copies_in = [pltpu.make_async_copy(a, b, sems.at[k]) for k, (a, b) in enumerate(zip(sources, targets))]
    matrix_copy = pltpu.make_async_copy(matrix_hbm, matrix_ref, sems.at[len(copies_in)])
    for copy in copies_in:
        copy.start()
    matrix_copy.start()
    for copy in copies_in:
        copy.wait()

    x = x_ref[...].reshape(depth * chain, features).astype(jnp.float32)
    center = x - jnp.mean(x, axis=-1, keepdims=True)
    spread = jnp.mean(center * center, axis=-1, keepdims=True)
    normed = center * lax.rsqrt(spread + 1e-05) * gain_ref[...] + offset_ref[...]
    normed = normed.astype(jnp.bfloat16)

    copies = LANES // width
    latter = latter_ref[...]
    former = former_ref[...]
    matrix = jnp.concatenate([latter] * copies + [former] * copies, axis=0)
    bias = jnp.concatenate([latter_bias_ref[...]] * copies + [former_bias_ref[...]] * copies, axis=1)
    both = lax.dot_general(normed, matrix, (((1,), (1,)), ((), ())), preferred_element_type=jnp.float32) + bias

    tallies = tallies_ref[...]
    lane_block = lax.broadcasted_iota(jnp.int32, (8, LANES), 1) // TILE
    for chunk in range(chain // LANES):
        lanes = slice(chunk * LANES, (chunk + 1) * LANES)
        across = jnp.broadcast_to(tallies[:, lanes], (LANES, LANES)).astype(jnp.float32)
        down = across.T
        down_ref[lanes] = down
        right_rows, left_rows = [], []
        for s in range(depth):
            row = (row_start + s).astype(jnp.float32)
            rows = slice(s * chain + chunk * LANES, s * chain + (chunk + 1) * LANES)
            right = both[rows, :LANES] * (row < down).astype(jnp.float32)
            left = both[rows, LANES:].T[:width] * (row < across[:width]).astype(jnp.float32)
            right_rows.append(right)
            left_rows.append(left)
        for b in range(LANES // TILE):
            tiles = []
            for s in range(depth):
                tile = None
                for q in range(copies):
                    part = right_rows[s][b * TILE + q * 8 : b * TILE + (q + 1) * 8]
                    tile = part if tile is None else jnp.where(lane_block == q, part, tile)
                tiles.append(tile)
            block = chunk * (LANES // TILE) + b
            right_ref[block * ROWS : (block + 1) * ROWS] = jnp.concatenate(tiles, 0).astype(jnp.bfloat16)
            tiles = []
            for s in range(depth):
                tile = None
                for q in range(copies):
                    part = left_rows[s][q * 8 : (q + 1) * 8]
                    shift = (q - b) * TILE % LANES
                    part = pltpu.roll(part, shift, 1) if shift else part
                    tile = part if tile is None else jnp.where(lane_block == q, part, tile)
                tiles.append(tile)
            left_ref[block * ROWS : (block + 1) * ROWS] = jnp.concatenate(tiles, 0).astype(jnp.bfloat16)

    right_unit = right_ref.shape[0] // split
    at = 0
    for kind, position in plan.own:
        source, index, unit = (left_ref, first, ROWS) if kind == "L" else (right_ref, second, right_unit)
        start = pl.multiple_of((index ^ position) * unit, ROWS)
        own_ref[at : at + unit] = source[pl.ds(start, unit)]
        at += unit
    for send_ref, (_, _, message) in zip(send_refs, plan.messages):
        at = 0
        for _, row, count in message:
            send_ref[at : at + count] = own_ref[row : row + count]
            at += count
    for out_ref, index in ((first_ref, first), (second_ref, second)):
        count = out_ref.shape[0]
        out_ref[...] = 1.0 / (down_ref[pl.ds(pl.multiple_of(index * count, TILE), count)] + 0.001)
    matrix_copy.wait()


def gathered(scratch_ref, buffers, tiles, block):
    for k, (buffer, row) in enumerate(tiles):
        start = pl.multiple_of(row + block * ROWS, ROWS)
        scratch_ref[k * ROWS : (k + 1) * ROWS] = buffers[buffer][pl.ds(start, ROWS)].astype(jnp.float32)


def stacked(scratch_ref, half, depth):
    return jnp.concatenate([scratch_ref[pl.ds(half * 4 + c, depth, stride=8)] for c in range(4)], 0)


def turns(scratch_ref, j8, depth):
    plain = scratch_ref[pl.ds(j8, depth, stride=8)]
    return [(pltpu.roll(plain, r * LANES // 4, 1) if r else plain).astype(jnp.bfloat16) for r in range(4)]


def ready_kernel(plan, blocks, *refs):
    buffers = refs[: plan.buffers - 1]
    matrix_ref, wide_ref, stack_ref, turned_ref, gather_ref = refs[plan.buffers - 1 :]
    sources = len(plan.left) // 2
    depth = sources * 2
    gathered(gather_ref, buffers, plan.left[:sources], 0)
    for half in range(2):
        stack_ref[half] = stacked(gather_ref, half, depth)
    matrix = matrix_ref[...]
    high = matrix.astype(jnp.bfloat16)
    wide_ref[:, :LANES] = high
    wide_ref[:, LANES:] = (matrix - high.astype(jnp.float32)).astype(jnp.bfloat16)

    def one_block(block, carry):
        gathered(gather_ref, buffers, plan.right[:sources], block)
        for j8 in range(8):
            for r, value in enumerate(turns(gather_ref, j8, depth)):
                turned_ref[block, j8 * 4 + r] = value
        return carry

    if blocks == 1:
        one_block(0, 0)
    else:
        lax.fori_loop(0, blocks, one_block, 0)


def pairs_kernel(plan, *refs):
    last_ref, wide_ref, stack_ref, turned_ref, first_ref, second_ref, out_ref = refs[:7]
    gather_left_ref, gather_ref, left_ref, outer_ref, done_ref, sems = refs[7:]
    first_count, second_count, _ = out_ref.shape
    sources = len(plan.left) // 2
    depth = sources * 2
    width = LANES // 4
    buffers = {plan.buffers - 1: last_ref}

    gathered(gather_left_ref, buffers, plan.left[sources:], 0)
    for half in range(2):
        rows = jnp.concatenate([stack_ref[half], stacked(gather_left_ref, half, depth)], 0)
        left_ref[half * LANES : (half + 1) * LANES] = rows.T.astype(jnp.bfloat16)
    first_scale = first_ref[...]

    def one_block(block, carry):
        gathered(gather_ref, buffers, plan.right[sources:], block)
        left = left_ref[...]
        lane_block = lax.broadcasted_iota(jnp.int32, (depth, LANES), 1) // width
        zero = jnp.zeros((depth, LANES), jnp.bfloat16)
        turned = [
            ([turned_ref[block, j8 * 4 + r] for r in range(4)], turns(gather_ref, j8, depth)) for j8 in range(8)
        ]

        def outer(q):
            for j8 in range(0, 8, 2):
                spread = jnp.concatenate(
                    [
                        jnp.concatenate(
                            [jnp.where(lane_block == c, t[(c - q) % 4], zero) for t in both for c in range(4)], 0
                        )
                        for both in turned[j8 : j8 + 2]
                    ],
                    1,
                )
                product = jnp.dot(left, spread, preferred_element_type=jnp.float32).astype(jnp.bfloat16)
                for at in range(2):
                    j = q * 8 + j8 + at
                    for half in range(2):
                        for gq in range(4):
                            rows = (half * 4 + gq) * TILE
                            group = gq * 2 + half
                            outer_ref[j * TILE : (j + 1) * TILE, group * LANES : (group + 1) * LANES] = (
                                product[rows : rows + TILE, at * LANES : (at + 1) * LANES]
                            )

        def project(q):
            rows = outer_ref[q * 8 * TILE : (q + 1) * 8 * TILE]
            projected = jnp.dot(rows, wide_ref[...], preferred_element_type=jnp.float32)
            projected = projected[:, :LANES] + projected[:, LANES:]
            start = pl.multiple_of(block * TILE + q * 8, 8)
            for k in range(8):
                scale = jnp.maximum(first_scale, second_ref[pl.ds(start + k, 1)])
                done_ref[q, pl.ds(k, first_count, stride=8)] = projected[k * TILE : (k + 1) * TILE] * scale
            return pltpu.make_async_copy(
                done_ref.at[q].reshape(first_count, 8, LANES), out_ref.at[:, pl.ds(start, 8)], sems.at[q]
            )

        outer(0)
        copies = []
        for q in range(4):
            if q + 1 < 4:
                outer(q + 1)
            copies.append(project(q))
            copies[-1].start()
        for copy in copies:
            copy.wait()
        return carry

    blocks = second_count // TILE
    if blocks == 1:
        one_block(0, 0)
    else:
        lax.fori_loop(0, blocks, one_block, 0)


def per_device(
    homolog_activations,
    homolog_tallies,
    standardize_gain,
    standardize_offset,
    former_factor_matrix,
    former_factor_offset,
    latter_factor_matrix,
    latter_factor_offset,
    pairwise_projection_matrix,
):
    depth, chain, features = homolog_activations.shape
    size_ri, size_rj, size_dp = (lax.axis_size(a) for a in ("ri", "rj", "dp"))
    split = size_rj * size_dp
    first_count, second_count = chain // size_ri, chain // split
    assert depth == 2 and first_count == TILE and second_count % TILE == 0 and chain % LANES == 0
    left_unit, right_unit = ROWS, ROWS * (second_count // TILE)
    total = size_ri * split
    bits = []
    bit = total // 2
    while bit >= size_dp:
        bits.append(bit)
        bit //= 2
    core = size_dp // 2
    stages = [[bits[0] | core]] if len(bits) % 2 else []
    bits = bits[len(bits) % 2 :]
    for high, low in zip(bits[::2], bits[1::2]):
        stages.append([low | core, high | core, low | high | core])
    if core:
        stages.append([core])
    plan = Plan(stages, split, left_unit, right_unit)
    sent = [sum(count for _, _, count in message) for stage, _, message in plan.messages if stage == 0]

    vmem = pl.BlockSpec(memory_space=pltpu.VMEM)
    bf16, f32 = jnp.bfloat16, jnp.float32
    operands = (
        homolog_activations,
        homolog_tallies[None, :],
        standardize_gain[None, :],
        standardize_offset[None, :],
        former_factor_matrix.T,
        former_factor_offset[None, :],
        latter_factor_matrix.T,
        latter_factor_offset[None, :],
    )
    in_hbm = [pltpu.with_memory_space_constraint(a, pltpu.HBM) for a in operands + (pairwise_projection_matrix,)]
    *own, first_scale, second_scale, matrix = pl.pallas_call(
        functools.partial(panels_kernel, plan, split),
        out_shape=(
            *(jax.ShapeDtypeStruct((rows, LANES), bf16) for rows in [plan.rows] + sent),
            jax.ShapeDtypeStruct((first_count, LANES), f32),
            jax.ShapeDtypeStruct((second_count, LANES), f32),
            jax.ShapeDtypeStruct(pairwise_projection_matrix.shape, f32),
        ),
        in_specs=[pl.BlockSpec(memory_space=pltpu.HBM)] * len(in_hbm),
        out_specs=(vmem,) * (4 + len(sent)),
        scratch_shapes=[pltpu.VMEM(a.shape, a.dtype) for a in operands]
        + [
            pltpu.VMEM((chain // TILE * ROWS, LANES), bf16),
            pltpu.VMEM((chain // TILE * ROWS, LANES), bf16),
            pltpu.VMEM((chain, LANES), f32),
            pltpu.SemaphoreType.DMA((len(in_hbm),)),
        ],
        compiler_params=pltpu.CompilerParams(vmem_limit_bytes=VMEM_BYTES),
        name="panels",
    )(*in_hbm)

    axes = ("ri", "rj", "dp")
    me = lax.axis_index(axes)
    move = lambda v, mask_of: lax.ppermute(v, axes, [(d, d ^ mask_of(d)) for d in range(total)])
    buffers = own[:1]
    for s, masks in enumerate(stages):
        if s == 0:
            messages = own[1:]
        else:
            messages = [
                jnp.concatenate([buffers[b][r : r + n] for b, r, n in message], 0)
                for stage, _, message in plan.messages
                if stage == s
            ]
        if len(masks) == 3:
            one, two, across = masks
            low, high = one & ~core, two & ~core
            even = lambda d: ((d & low) != 0) == ((d & high) != 0)
            messages = [
                jnp.where(even(me), messages[1], messages[0]),
                jnp.where(even(me), messages[0], messages[1]),
                messages[2],
            ]
            messages = list(lax.optimization_barrier(tuple(messages)))
            ways = [lambda d: two if even(d) else one, lambda d: one if even(d) else two, lambda d: across]
        else:
            ways = [lambda d: masks[0]]
        buffers = buffers + [move(v, way) for v, way in zip(messages, ways)]

    blocks, sources = second_count // TILE, total // 2
    wide, stack, turned = pl.pallas_call(
        functools.partial(ready_kernel, plan, blocks),
        out_shape=(
            jax.ShapeDtypeStruct((8 * LANES, 2 * LANES), bf16),
            jax.ShapeDtypeStruct((2, 8 * sources, LANES), f32),
            jax.ShapeDtypeStruct((blocks, 32, 2 * sources, LANES), bf16),
        ),
        in_specs=[vmem] * plan.buffers,
        out_specs=(vmem,) * 3,
        scratch_shapes=[pltpu.VMEM((sources * ROWS, LANES), f32)],
        compiler_params=pltpu.CompilerParams(vmem_limit_bytes=VMEM_BYTES),
        name="ready",
    )(*buffers[:-1], matrix)
    return pl.pallas_call(
        functools.partial(pairs_kernel, plan),
        out_shape=jax.ShapeDtypeStruct((first_count, second_count, LANES), f32),
        in_specs=[vmem] * 6,
        out_specs=pl.BlockSpec(memory_space=pl.ANY),
        scratch_shapes=[
            pltpu.VMEM((sources * ROWS, LANES), f32),
            pltpu.VMEM((sources * ROWS, LANES), f32),
            pltpu.VMEM((2 * LANES, 4 * total * 2), bf16),
            pltpu.VMEM((first_count * TILE, 8 * LANES), bf16),
            pltpu.VMEM((4, first_count * 8, LANES), f32),
            pltpu.SemaphoreType.DMA((4,)),
        ],
        compiler_params=pltpu.CompilerParams(vmem_limit_bytes=VMEM_BYTES),
        name="pairs",
    )(buffers[-1], wide, stack, turned, first_scale, second_scale)


def solution(mesh):
    placed = (P(("grp", "ri", "rj", "dp"), None, None), P("grp"), P(), P(), P(), P(), P(), P(), P())
    return jax.shard_map(
        per_device,
        mesh=mesh,
        in_specs=placed,
        out_specs=P(("grp", "ri"), ("rj", "dp"), None),
        check_vma=False,
    )
```
